256 devices in a mesh: ctx: 128 (over x_lo, z, y, core), tp: 2 (over x_hi).
Axes of the slice: x: 4 (x_hi: 2, x_lo: 2; x = x_hi * 2 + x_lo), y: 4, z: 8, core: 2. Of those that a mesh axis runs over, the one named last changes fastest.
Arguments:
- video_query: bfloat16 [32768, 3072], P('ctx', 'tp'), may hold values from -400 to 400
- video_key: bfloat16 [32768, 3072], P('ctx', 'tp'), may hold values from -400 to 400
- video_value: bfloat16 [32768, 3072], P('ctx', 'tp'), may hold values from -6 to 6
- audio_query: bfloat16 [512, 3072], P('ctx', 'tp'), may hold values from -400 to 400
- audio_key: bfloat16 [512, 3072], P('ctx', 'tp'), may hold values from -400 to 400
- audio_value: bfloat16 [512, 3072], P('ctx', 'tp'), may hold values from -6 to 6
- video_query_gain: float32 [3072], P('tp'), may hold values from 0.7 to 4.5
- video_key_gain: float32 [3072], P('tp'), may hold values from 0.7 to 4.5
- audio_query_gain: float32 [3072], P('tp'), may hold values from 0.7 to 4.5
- audio_key_gain: float32 [3072], P('tp'), may hold values from 0.7 to 4.5
- tile_flags: int32 [128, 3], P('ctx'), may hold values 0 or 1
- audio_centers: int32 [128], P('ctx'), may hold values from 0 to 511, as said below
- out_grad: bfloat16 [32768, 3072], P('ctx', 'tp'), may hold values from -6 to 6
Outputs:
- video_out: bfloat16 [32768, 3072], P('ctx', 'tp')
- audio_out: bfloat16 [512, 3072], P('ctx', 'tp')
- grad_query: bfloat16 [32768, 3072], P('ctx', 'tp')
- grad_key: bfloat16 [32768, 3072], P('ctx', 'tp')
- grad_value: bfloat16 [32768, 3072], P('ctx', 'tp')
The draws below stay inside these ranges and needn't reach their ends.
Inputs may be any that keep to these rules, and one draw needn't show every extreme that they name: audio_centers[b] lies within 4 of b * 4 + 4 // 2; the first is 0 and the last 511.
All inputs are finite; a program needn't handle non-finite values. No bound on the sum of `tile_flags` on one device may be relied on, other than what follows from the above.
Results may differ from the reference program's by a relative error of at most 0.01105.
The reference program's roundings to bfloat16 on the way count: a program that leaves them out, or rounds other values in their place, can miss the bound.
Values may be sent and summed in bfloat16 or wider, within the bound.
No kernel may reach another device: no remote copies, remote signals or barrier semaphores. Data moves between devices by JAX's collectives and lax.ppermute only.
A program may use at most 128 MiB of HBM per device.

```python
import math
import jax
import jax.numpy as jnp
from jax import lax

D = 3072
HEADS = 24
HEAD_WIDTH = 128
VIDEO_BLOCK_ROWS = 256
A_DEV = 4
BLOCKS_BACK = 3
VIDEO_BLOCKS = 128
VIDEO = 32768
AUDIO = 512
AUD_REACH = 8


def rough_rows(key, row_total, column_rise):
    normal_part = jnp.clip(jax.random.normal(jax.random.fold_in(key, 1), (row_total, D)), -4.0, 4.0)
    mixed = normal_part
    row_scale = jnp.exp(jax.random.uniform(jax.random.fold_in(key, 4), (row_total, 1), minval=0.0, maxval=2.3))
    col_scale = jnp.exp(column_rise * jnp.arange(D, dtype=jnp.float32) / D)
    return mixed * row_scale * col_scale


def gain_values(key, lowest, highest):
    return jnp.exp(jax.random.uniform(key, (D,), minval=math.log(lowest), maxval=math.log(highest)))


def draw_video_query(key, part):
    key = jax.random.fold_in(key, 11)
    values = rough_rows(key, VIDEO, 2.3)
    return values.astype(jnp.bfloat16)


def draw_video_key(key, part):
    key = jax.random.fold_in(key, 12)
    values = rough_rows(key, VIDEO, 2.3)
    return values.astype(jnp.bfloat16)


def draw_audio_query(key, part):
    key = jax.random.fold_in(key, 13)
    values = rough_rows(key, AUDIO, 2.3)
    return values.astype(jnp.bfloat16)


def draw_audio_key(key, part):
    key = jax.random.fold_in(key, 14)
    values = rough_rows(key, AUDIO, 2.3)
    return values.astype(jnp.bfloat16)


def draw_video_query_gain(key, part):
    key = jax.random.fold_in(key, 21)
    return gain_values(key, 0.7, 2.5)


def draw_video_key_gain(key, part):
    key = jax.random.fold_in(key, 22)
    return gain_values(key, 0.7, 2.5)


def draw_audio_query_gain(key, part):
    key = jax.random.fold_in(key, 23)
    return gain_values(key, 0.7, 2.5)


def draw_audio_key_gain(key, part):
    key = jax.random.fold_in(key, 24)
    return gain_values(key, 0.7, 2.5)


def draw_audio_centers(key, part):
    key = jax.random.fold_in(key, 41)
    block_ids = jnp.arange(VIDEO_BLOCKS, dtype=jnp.int32)
    jitter = jax.random.randint(key, (VIDEO_BLOCKS,), -A_DEV, A_DEV + 1).astype(jnp.int32)
    centers = jnp.clip(block_ids * A_DEV + A_DEV // 2 + jitter, 0, AUDIO - 1)
    centers = jnp.where(block_ids == 0, 0, centers)
    centers = jnp.where(block_ids == VIDEO_BLOCKS - 1, AUDIO - 1, centers)
    return centers.astype(jnp.int32)


def with_ends(entries, stream_key, low, top_value):
    longest = entries.shape.index(max(entries.shape))
    spots = []
    for shift in (0, 1):
        where = [jax.random.randint(jax.random.fold_in(stream_key, axis), (), 0, length) for axis, length in enumerate(entries.shape)]
        where[longest] = (where[longest] + shift) % entries.shape[longest]
        spots.append(tuple(where))
    return entries.at[spots[0]].set(low).at[spots[1]].set(top_value)


def levels(stream_key, shape, cuts, smallest, largest):
    factor_of, own = 1.0, jax.random.fold_in(stream_key, 6)
    for dim, blocks in cuts:
        draws = jnp.exp(jax.random.uniform(jax.random.fold_in(own, dim), (blocks,), jnp.float32, smallest / len(cuts), largest / len(cuts)))
        factor_of = factor_of * jnp.repeat(draws, shape[dim] // blocks).reshape([-1 if axis == dim else 1 for axis in range(len(shape))])
    return factor_of


def normal_values(key, dims, scale, limit, cuts=(), held_as=jnp.bfloat16):
    values = scale * jax.random.normal(key, dims, jnp.float32)
    if cuts:
        values = values * levels(key, dims, cuts, -0.22, 0.18)
    return jnp.clip(values, -limit, limit).astype(held_as)


def setup_inputs(seed: int = 0) -> dict:
    keys = jax.random.split(jax.random.key(seed), 14)
    return {
        "video_query": draw_video_query(jax.random.fold_in(keys[13], 71), 0),
        "video_key": draw_video_key(jax.random.fold_in(keys[13], 71), 0),
        "video_value": normal_values(keys[2], (VIDEO, D), 1.0, 6.0, ((0, 128), (1, 2))),
        "audio_query": draw_audio_query(jax.random.fold_in(keys[13], 71), 0),
        "audio_key": draw_audio_key(jax.random.fold_in(keys[13], 71), 0),
        "audio_value": normal_values(keys[5], (AUDIO, D), 1.0, 6.0, ((0, 128), (1, 2))),
        "video_query_gain": draw_video_query_gain(jax.random.fold_in(keys[13], 71), 0),
        "video_key_gain": draw_video_key_gain(jax.random.fold_in(keys[13], 71), 0),
        "audio_query_gain": draw_audio_query_gain(jax.random.fold_in(keys[13], 71), 0),
        "audio_key_gain": draw_audio_key_gain(jax.random.fold_in(keys[13], 71), 0),
        "tile_flags": with_ends((jax.random.randint(keys[10], (VIDEO_BLOCKS, BLOCKS_BACK), 0, 2) < 1).astype(jnp.int32), jax.random.fold_in(keys[10], 1), 0, 1),
        "audio_centers": draw_audio_centers(jax.random.fold_in(keys[13], 71), 0),
        "out_grad": normal_values(keys[12], (VIDEO, D), 1.0, 6.0, ((0, 128), (1, 2))),
    }


EPSILON = 1e-06
MASKED = -1e+30

def row_factor(values):
    energy = lax.optimization_barrier(jnp.sum(jnp.square(values.astype(jnp.float32)), axis=1))
    return lax.rsqrt(energy / D + EPSILON)

def normed(values, factor, scaling):
    return (values.astype(jnp.float32) * factor[:, None] * scaling).astype(jnp.bfloat16)

def split_heads(values):
    return values.reshape(values.shape[0], HEADS, HEAD_WIDTH).astype(jnp.float32)

def head_logits(queries, key_rows):
    return jnp.einsum('qhd,khd->hqk', queries, key_rows) * HEAD_WIDTH ** (-0.5)

def softmax_rows(logits, allowed):
    logits = jnp.where(allowed, logits, MASKED)
    maximum = lax.optimization_barrier(jnp.max(logits, axis=-1, keepdims=True))
    attention_weights = jnp.exp(logits - maximum)
    totals = lax.optimization_barrier(jnp.sum(attention_weights, axis=-1, keepdims=True))
    return (attention_weights / totals, maximum[..., 0], totals[..., 0])

def rounded_probs(values):
    return lax.optimization_barrier(values.astype(jnp.bfloat16)).astype(jnp.float32)

def norm_back(values, factor, scaling, dnormed):
    widened = values.astype(jnp.float32)
    inner_sum = lax.optimization_barrier(jnp.sum(widened * scaling * dnormed, axis=1, keepdims=True))
    result = factor[:, None] * scaling * dnormed - widened * factor[:, None] ** 3 * inner_sum / D
    return result.astype(jnp.bfloat16)

def reference(video_query, video_key, video_value, audio_query, audio_key, audio_value, video_query_gain, video_key_gain, audio_query_gain, audio_key_gain, tile_flags, audio_centers, out_grad):
    logit_scale = HEAD_WIDTH ** (-0.5)
    query_factor = row_factor(video_query)
    key_factor = row_factor(video_key)
    query_n = normed(video_query, query_factor, video_query_gain)
    key_n = normed(video_key, key_factor, video_key_gain)
    audio_query_n = normed(audio_query, row_factor(audio_query), audio_query_gain)
    audio_key_n = normed(audio_key, row_factor(audio_key), audio_key_gain)
    margin = BLOCKS_BACK * VIDEO_BLOCK_ROWS
    key_padded = jnp.concatenate([jnp.zeros((margin, D), jnp.bfloat16), key_n], axis=0)
    value_padded = jnp.concatenate([jnp.zeros((margin, D), jnp.bfloat16), video_value], axis=0)
    audio_keys = split_heads(audio_key_n)
    audio_values = split_heads(audio_value)
    positions = jnp.arange(AUDIO, dtype=jnp.int32)
    lookback = jnp.arange(BLOCKS_BACK + 1, dtype=jnp.int32)

    def forward_block(block_id):
        first_row = (block_id * VIDEO_BLOCK_ROWS).astype(jnp.int32)
        queries = split_heads(lax.dynamic_slice_in_dim(query_n, first_row, VIDEO_BLOCK_ROWS, 0))
        cotangent = split_heads(lax.dynamic_slice_in_dim(out_grad, first_row, VIDEO_BLOCK_ROWS, 0))
        key_rows = split_heads(lax.dynamic_slice_in_dim(key_padded, first_row, margin + VIDEO_BLOCK_ROWS, 0))
        value_rows = split_heads(lax.dynamic_slice_in_dim(value_padded, first_row, margin + VIDEO_BLOCK_ROWS, 0))
        source = block_id - BLOCKS_BACK + lookback
        distance = block_id - source - 1
        flagged = jnp.take(tile_flags[block_id], jnp.clip(distance, 0, BLOCKS_BACK - 1))
        tile_live = jnp.where(distance < 0, 1, flagged * (source >= 0).astype(jnp.int32))
        key_live = jnp.repeat(tile_live, VIDEO_BLOCK_ROWS, total_repeat_length=margin + VIDEO_BLOCK_ROWS) > 0
        self_shares, maximum, totals = softmax_rows(head_logits(queries, key_rows), key_live[None, None, :])
        self_out = jnp.einsum('hqk,khd->qhd', rounded_probs(self_shares), value_rows)
        linked = jnp.abs(positions - audio_centers[block_id]) <= AUD_REACH
        cross_shares = softmax_rows(head_logits(queries, audio_keys), linked[None, None, :])[0]
        cross_out = jnp.einsum('hqk,khd->qhd', rounded_probs(cross_shares), audio_values)
        video_rows = (self_out + cross_out).reshape(VIDEO_BLOCK_ROWS, D).astype(jnp.bfloat16)
        self_dot = lax.optimization_barrier(jnp.sum(cotangent * self_out, axis=-1)).T
        self_dlogit = rounded_probs(self_shares * (jnp.einsum('qhd,khd->hqk', cotangent, value_rows) - self_dot[:, :, None]))
        cross_dot = lax.optimization_barrier(jnp.sum(cotangent * cross_out, axis=-1)).T
        cross_dlogit = rounded_probs(cross_shares * (jnp.einsum('qhd,khd->hqk', cotangent, audio_values) - cross_dot[:, :, None]))
        query_dn = (jnp.einsum('hqk,khd->qhd', self_dlogit, key_rows) + jnp.einsum('hqk,khd->qhd', cross_dlogit, audio_keys)) * logit_scale
        return (video_rows, query_dn.reshape(VIDEO_BLOCK_ROWS, D), maximum, totals, self_dot)
    block_ids = jnp.arange(VIDEO_BLOCKS, dtype=jnp.int32)
    video_out, query_dn, maxima, totals_all, self_dots = lax.map(forward_block, block_ids)
    video_out = video_out.reshape(VIDEO, D)
    query_dn = query_dn.reshape(VIDEO, D)

    def key_block(block_id):
        first_row = (block_id * VIDEO_BLOCK_ROWS).astype(jnp.int32)
        key_rows = split_heads(lax.dynamic_slice_in_dim(key_n, first_row, VIDEO_BLOCK_ROWS, 0))
        value_rows = split_heads(lax.dynamic_slice_in_dim(video_value, first_row, VIDEO_BLOCK_ROWS, 0))
        key_sum = jnp.zeros((VIDEO_BLOCK_ROWS, HEADS, HEAD_WIDTH), jnp.float32)
        value_sum = jnp.zeros((VIDEO_BLOCK_ROWS, HEADS, HEAD_WIDTH), jnp.float32)
        for offset in range(-1, BLOCKS_BACK):
            target = block_id + 1 + offset
            clamped = jnp.minimum(target, VIDEO_BLOCKS - 1).astype(jnp.int32)
            if offset < 0:
                tile_on = (target < VIDEO_BLOCKS).astype(jnp.int32)
            else:
                tile_on = tile_flags[clamped, offset] * (target < VIDEO_BLOCKS).astype(jnp.int32)
            query_row = (clamped * VIDEO_BLOCK_ROWS).astype(jnp.int32)
            queries = split_heads(lax.dynamic_slice_in_dim(query_n, query_row, VIDEO_BLOCK_ROWS, 0))
            cotangent = split_heads(lax.dynamic_slice_in_dim(out_grad, query_row, VIDEO_BLOCK_ROWS, 0))
            logits = head_logits(queries, key_rows)
            shares = jnp.where(tile_on > 0, jnp.exp(logits - maxima[clamped][:, :, None]) / totals_all[clamped][:, :, None], 0.0)
            dlogit = rounded_probs(shares * (jnp.einsum('qhd,khd->hqk', cotangent, value_rows) - self_dots[clamped][:, :, None]))
            key_term = jnp.einsum('hqk,qhd->khd', dlogit, queries) * logit_scale
            value_term = jnp.einsum('hqk,qhd->khd', rounded_probs(shares), cotangent)
            if offset < 0:
                key_sum = key_term
                value_sum = value_term
            else:
                key_sum = key_sum + rounded_probs(key_term)
                value_sum = value_sum + rounded_probs(value_term)
        return (key_sum.reshape(VIDEO_BLOCK_ROWS, D), value_sum.reshape(VIDEO_BLOCK_ROWS, D))
    key_dn, value_grad = lax.map(key_block, block_ids)
    key_dn = key_dn.reshape(VIDEO, D)
    grad_value = value_grad.reshape(VIDEO, D).astype(jnp.bfloat16)
    grad_query = norm_back(video_query, query_factor, video_query_gain, query_dn)
    grad_key = norm_back(video_key, key_factor, video_key_gain, key_dn)
    block_linked = jnp.abs(positions[:, None] - audio_centers[None, :]) <= AUD_REACH

    def audio_head(head_id):
        first_col = (head_id * HEAD_WIDTH).astype(jnp.int32)
        head_query = lax.dynamic_slice_in_dim(audio_query_n, first_col, HEAD_WIDTH, 1)
        head_key = lax.dynamic_slice_in_dim(key_n, first_col, HEAD_WIDTH, 1)
        head_value_rows = lax.dynamic_slice_in_dim(video_value, first_col, HEAD_WIDTH, 1)
        logits = jnp.dot(head_query, head_key.T, preferred_element_type=jnp.float32) * logit_scale
        logits = logits.reshape(AUDIO, VIDEO_BLOCKS, VIDEO_BLOCK_ROWS)
        logits = jnp.where(block_linked[:, :, None], logits, MASKED)
        block_peak = lax.optimization_barrier(jnp.max(logits, axis=2))
        attention_weights = jnp.where(block_linked[:, :, None], jnp.exp(logits - block_peak[:, :, None]), 0.0)
        block_mass = lax.optimization_barrier(jnp.sum(attention_weights, axis=2))
        block_total_sum = jnp.einsum('rlf,lfx->rlx', rounded_probs(attention_weights), head_value_rows.reshape(VIDEO_BLOCKS, VIDEO_BLOCK_ROWS, HEAD_WIDTH).astype(jnp.float32))
        top = lax.optimization_barrier(jnp.max(block_peak, axis=1, keepdims=True))
        ratios = jnp.exp(block_peak - top)
        summed = lax.optimization_barrier(jnp.sum(ratios[:, :, None] * block_total_sum, axis=1))
        mass_sum = lax.optimization_barrier(jnp.sum(ratios * block_mass, axis=1))
        return summed / mass_sum[:, None]
    per_head = lax.map(audio_head, jnp.arange(HEADS, dtype=jnp.int32))
    audio_out = jnp.transpose(per_head, (1, 0, 2)).reshape(AUDIO, D).astype(jnp.bfloat16)
    return (video_out, audio_out, grad_query, grad_key, grad_value)
```

```python
import math

import jax
import jax.numpy as jnp
from jax import lax
from jax.experimental import pallas as pl
from jax.experimental.pallas import tpu as pltpu
from jax.sharding import PartitionSpec as P

D = 3072
HEADS = 24
HEAD_WIDTH = 128
AUD_REACH = 8
EPSILON = 1e-06
MASKED = -1e30
BACK = 3
ROWS = 256
AUDIO_ROWS = 4
AUDIO_BLOCK = 16
PAYLOAD = 2 * ROWS + AUDIO_BLOCK
SCALE = HEAD_WIDTH ** (-0.5)
SCALE2 = SCALE * math.log2(math.e)
F32 = jnp.float32
BF16 = jnp.bfloat16
VMEM_LIMIT = 48 * 1024 * 1024

EVEN, LIVE, BLOCK, CENTER, AHEAD, TOTAL_AUDIO = 0, 1, 4, 5, 6, 9

VMEM = pl.BlockSpec(memory_space=pltpu.VMEM)
SMEM = pl.BlockSpec(memory_space=pltpu.SMEM)
ANY = pl.BlockSpec(memory_space=pl.ANY)


def cols(head):
    return slice(head * HEAD_WIDTH, (head + 1) * HEAD_WIDTH)


def dot_nt(a, b):
    return lax.dot_general(a, b, (((1,), (1,)), ((), ())), preferred_element_type=F32)


def dot_nn(a, b):
    return lax.dot_general(a, b, (((1,), (0,)), ((), ())), preferred_element_type=F32)


def call(kernel, outs, ins, scratch=(), flops=0, nbytes=0, name=None):
    return pl.pallas_call(
        kernel,
        out_shape=[jax.ShapeDtypeStruct(s, d) for s, d in outs],
        in_specs=ins,
        out_specs=[VMEM] * len(outs),
        scratch_shapes=list(scratch),
        compiler_params=pltpu.CompilerParams(vmem_limit_bytes=VMEM_LIMIT),
        cost_estimate=pl.CostEstimate(flops=flops, bytes_accessed=nbytes, transcendentals=0),
        name=name,
    )


class Pick:
    def __init__(self, even, when_even, when_odd, target, sem):
        self.even, self.pair, self.target, self.sem = even, (when_even, when_odd), target, sem

    def start(self):
        @pl.when(self.even)
        def _():
            pltpu.make_async_copy(self.pair[0], self.target, self.sem).start()

        @pl.when(jnp.logical_not(self.even))
        def _():
            pltpu.make_async_copy(self.pair[1], self.target, self.sem).start()
        return self

    def wait(self):
        pltpu.make_async_copy(self.pair[0], self.target, self.sem).wait()


def lane_sums(wide):
    return jnp.sum(wide.T, axis=0, keepdims=True)


def as_rows(lanes):
    return jnp.broadcast_to(lanes, (HEAD_WIDTH, lanes.shape[1])).T


def energy_kernel(q, k, a, out, scr):
    heads = q.shape[1] // HEAD_WIDTH

    def squares(ref):
        total = None
        for h in range(heads):
            v = ref[:, cols(h)].astype(F32)
            total = v * v if total is None else total + v * v
        return total

    out[...] = jnp.zeros_like(out)
    out[0:1, :] = lane_sums(squares(q))
    out[1:2, :] = lane_sums(squares(k))
    scr[...] = jnp.zeros_like(scr)
    scr[0:AUDIO_BLOCK, :] = squares(a)
    out[2:3, 0:128] = lane_sums(scr[...])


def factors(e0, e1):
    return lax.rsqrt((e0[...] + e1[...]) / D + EPSILON)


def prep_kernel(info, q, k, v, g, a, e0, e1, gq, gk, gaq, gak, link, chip):
    heads = q.shape[1] // HEAD_WIDTH
    f = factors(e0, e1)
    fq, fk = as_rows(f[0:1]), as_rows(f[1:2])
    row = lax.broadcasted_iota(jnp.int32, (AUDIO_BLOCK, 128), 0)
    is_key, is_query = row < 4, (row >= 8) & (row < 12)
    fa = jnp.where(is_key | is_query, as_rows(f[2:3, 0:128])[0:AUDIO_BLOCK], 1.0)

    def fill(kv, qd):
        for h in range(heads):
            c = cols(h)
            kv[0:ROWS, c] = (k[:, c].astype(F32) * fk * gk[:, c]).astype(BF16)
            kv[ROWS : 2 * ROWS, c] = v[:, c]
            qd[0:ROWS, c] = (q[:, c].astype(F32) * fq * gq[:, c]).astype(BF16)
            qd[ROWS : 2 * ROWS, c] = g[:, c]
            ga = jnp.where(is_key, gak[:, c], jnp.where(is_query, gaq[:, c], 1.0))
            audio = (a[:, c].astype(F32) * fa * ga).astype(BF16)
            kv[2 * ROWS :, c] = audio
            qd[2 * ROWS :, c] = audio

    @pl.when(info[EVEN] == 1)
    def _():
        fill(chip, link)

    @pl.when(info[EVEN] == 0)
    def _():
        fill(link, chip)


def audio_tile(queries, keys, values, linked):
    x = dot_nt(queries, keys) * SCALE2
    peak = jnp.max(x, axis=1, keepdims=True)
    w = jnp.exp2(x - peak)
    mass = jnp.sum(w, axis=1, keepdims=True)
    mean = dot_nn(w.astype(BF16), values) / mass
    weight = jnp.where(linked, peak + jnp.log2(mass), MASKED)
    return mean, weight


def audio_linked(rows, block, distance, relative):
    token = lax.broadcasted_iota(jnp.int32, (rows, 1), 0) % AUDIO_BLOCK - 8
    ok = (token >= 0) & (token < AUDIO_ROWS) & (block - distance >= 0)
    gap = (token + 4 * distance - 2).astype(F32) - relative
    return ok & (jnp.abs(gap) <= AUD_REACH)


def mid_kernel(info, xl, xc, l1, c1, l2, c2, c3, t3,
               o_out, ml_out, cross_out, dqx_out, own_out, m1, m2, m3,
               qd, kv0, kv1, kv2, aw, sems):
    heads = qd.shape[1] // HEAD_WIDTH
    even = info[EVEN] == 1
    block = info[BLOCK]
    tail = pl.ds(2 * ROWS, AUDIO_BLOCK)

    def seat(j):
        return aw.at[pl.ds(AUDIO_BLOCK * j, AUDIO_BLOCK)]

    a_rows = lambda ref: ref.at[tail]
    copies = [
        Pick(even, xl, xc, qd, sems.at[0]),
        Pick(even, xc, xl, kv0, sems.at[1]),
        Pick(even, l1, c1, kv1, sems.at[2]),
        Pick(even, l2, c2, kv2, sems.at[3]),
        Pick(even, t3, a_rows(c3), seat(0), sems.at[4]),
        Pick(even, a_rows(l2), a_rows(c2), seat(1), sems.at[5]),
        Pick(even, a_rows(l1), a_rows(c1), seat(2), sems.at[6]),
        Pick(even, a_rows(xl), a_rows(xl), seat(3), sems.at[7]),
        Pick(even, a_rows(c1), a_rows(l1), seat(4), sems.at[8]),
        Pick(even, a_rows(c2), a_rows(l2), seat(5), sems.at[9]),
        Pick(even, a_rows(c3), t3, seat(6), sems.at[10]),
    ]
    for copy in copies:
        copy.start()
    aw[112:128, :] = jnp.zeros((AUDIO_BLOCK, aw.shape[1]), BF16)
    ml_out[...] = jnp.zeros_like(ml_out)
    for copy in copies:
        copy.wait()

    live = [None, info[LIVE] == 1, info[LIVE + 1] == 1]
    lane = lax.broadcasted_iota(jnp.int32, (1, 128), 1)
    token = lane % AUDIO_BLOCK
    position = (block - BACK + lane // AUDIO_BLOCK) * AUDIO_ROWS + token
    linked = (
        (token < AUDIO_ROWS) & (lane < 112) & (position >= 0) & (position < info[TOTAL_AUDIO])
        & (jnp.abs(position - info[CENTER]) <= AUD_REACH)
    )
    seat_row = lax.broadcasted_iota(jnp.int32, (64, 1), 0)
    token_row = seat_row % AUDIO_BLOCK - 8
    position_row = (block - BACK + seat_row // AUDIO_BLOCK) * AUDIO_ROWS + token_row
    linked_rows = (
        (token_row >= 0) & (token_row < AUDIO_ROWS) & (position_row >= 0)
        & (jnp.abs(position_row - info[CENTER]) <= AUD_REACH)
    )
    relative = [None] + [
        aw[AUDIO_BLOCK * (3 - d) : AUDIO_BLOCK * (4 - d), 0:128].astype(F32)[12:13, 0:1] for d in (1, 2)
    ]
    own_linked = [None] + [audio_linked(AUDIO_BLOCK, block, d, relative[d]) for d in (1, 2)]

    for h in range(heads):
        c = cols(h)
        q, g = qd[0:ROWS, c], qd[ROWS : 2 * ROWS, c]
        scores = []
        for t, kv in enumerate((kv0, kv1, kv2)):
            s = dot_nt(q, kv[0:ROWS, c])
            scores.append(s if t == 0 else jnp.where(live[t], s, MASKED))
        peak = scores[0]
        for s in scores[1:]:
            peak = jnp.maximum(peak, s)
        peak = jnp.max(peak, axis=1, keepdims=True)
        total, out = None, None
        for s, kv in zip(scores, (kv0, kv1, kv2)):
            p = jnp.exp2((s - peak) * SCALE2)
            total = p if total is None else total + p
            term = dot_nn(p.astype(BF16), kv[ROWS : 2 * ROWS, c])
            out = term if out is None else out + term
        o_out[:, c] = out
        ml_out[:, h : h + 1] = peak
        ml_out[:, 16 + h : 17 + h] = jnp.sum(total, axis=1, keepdims=True)
        ak = aw[:, c]
        av = pltpu.roll(ak.astype(F32), 124, 0).astype(BF16)
        s = jnp.where(linked, dot_nt(q, ak), MASKED)
        p = jnp.exp2((s - jnp.max(s, axis=1, keepdims=True)) * SCALE2)
        share = p / jnp.sum(p, axis=1, keepdims=True)
        cross = dot_nn(share.astype(BF16), av)
        cross_out[:, c] = cross
        dot_row = jnp.sum(g.astype(F32) * cross, axis=1, keepdims=True)
        dlogit = (share * (dot_nt(g, av) - dot_row)).astype(BF16)
        dqx_out[:, c] = dot_nn(dlogit, ak)
        mean, weight = audio_tile(ak[0:64], kv0[0:ROWS, c], kv0[ROWS : 2 * ROWS, c], linked_rows)
        weight = jnp.broadcast_to(weight, mean.shape)
        for msg, j in ((m3, 0), (m2, 1), (m1, 2)):
            r = slice(AUDIO_BLOCK * j + 8, AUDIO_BLOCK * j + 12)
            msg[0:4, c] = mean[r]
            msg[4:8, c] = weight[r]
        means, weights = [mean[48:64]], [weight[48:64]]
        for d, kv in ((1, kv1), (2, kv2)):
            mean, weight = audio_tile(ak[48:64], kv[0:ROWS, c], kv[ROWS : 2 * ROWS, c], own_linked[d])
            means.append(mean)
            weights.append(jnp.broadcast_to(weight, mean.shape))
        top = jnp.maximum(jnp.maximum(weights[0], weights[1]), weights[2])
        ratios = [jnp.exp2(w - top) for w in weights]
        mass = ratios[0] + ratios[1] + ratios[2]
        mean = (ratios[0] * means[0] + ratios[1] * means[1] + ratios[2] * means[2]) / mass
        own_out[0:4, c] = mean[8:12]
        own_out[4:8, c] = (top + jnp.log2(mass))[8:12]


def last_kernel(info, xl, xc, l3, c3, o_in, ml_in, cross_in,
                video, stat, s1, s2, s3, qd, kv3, sems):
    heads = qd.shape[1] // HEAD_WIDTH
    even = info[EVEN] == 1
    copies = [Pick(even, xl, xc, qd, sems.at[0]).start(), Pick(even, l3, c3, kv3, sems.at[1]).start()]
    stat[...] = jnp.zeros_like(stat)
    for copy in copies:
        copy.wait()
    live = info[LIVE + 2] == 1
    for h in range(heads):
        c = cols(h)
        q, g = qd[0:ROWS, c], qd[ROWS : 2 * ROWS, c]
        s = jnp.where(live, dot_nt(q, kv3[0:ROWS, c]), MASKED)
        before = ml_in[:, h : h + 1]
        peak = jnp.maximum(before, jnp.max(s, axis=1, keepdims=True))
        decay = jnp.exp2((before - peak) * SCALE2)
        p = jnp.exp2((s - peak) * SCALE2)
        mass = ml_in[:, 16 + h : 17 + h] * decay + jnp.sum(p, axis=1, keepdims=True)
        out = o_in[:, c] * decay + dot_nn(p.astype(BF16), kv3[ROWS : 2 * ROWS, c])
        out = out / mass
        video[:, c] = (out + cross_in[:, c]).astype(BF16)
        stat[:, h : h + 1] = peak * SCALE2 + jnp.log2(mass)
        stat[:, 16 + h : 17 + h] = jnp.sum(g.astype(F32) * out, axis=1, keepdims=True)
    rows = stat[...].T[0:32]
    index = lax.broadcasted_iota(jnp.int32, rows.shape, 0)
    for s, msg in enumerate((s1, s2, s3)):
        msg[...] = jnp.where((index < 16) & (info[LIVE + s] == 0), -MASKED, rows)


def query_kernel(info, xl, xc, l1, c1, l2, c2, l3, c3, dqx, stat, q_raw, gain,
                 dq_out, inner, own_out, qd, kv0, kv1, kv2, kv3, sems):
    heads = qd.shape[1] // HEAD_WIDTH
    even = info[EVEN] == 1
    copies = [
        Pick(even, xl, xc, qd, sems.at[0]),
        Pick(even, xc, xl, kv0, sems.at[1]),
        Pick(even, l1, c1, kv1, sems.at[2]),
        Pick(even, l2, c2, kv2, sems.at[3]),
        Pick(even, l3, c3, kv3, sems.at[4]),
    ]
    for copy in copies:
        copy.start()
    copies[0].wait()

    def tile(kv):
        for h in range(heads):
            c = cols(h)
            q, g, k, v = qd[0:ROWS, c], qd[ROWS : 2 * ROWS, c], kv[0:ROWS, c], kv[ROWS : 2 * ROWS, c]
            p = jnp.exp2(dot_nt(q, k) * SCALE2 - stat[:, h : h + 1])
            dlogit = (p * (dot_nt(g, v) - stat[:, 16 + h : 17 + h])).astype(BF16)
            before = dqx[:, c] if kv is kv0 else dq_out[:, c]
            dq_out[:, c] = before + dot_nn(dlogit, k)

    copies[1].wait()
    tile(kv0)
    for t, kv in ((1, kv1), (2, kv2), (3, kv3)):
        copies[1 + t].wait()

        @pl.when(info[LIVE + t - 1] == 1)
        def _():
            tile(kv)

    acc = None
    for h in range(heads):
        c = cols(h)
        dq = dq_out[:, c] * SCALE
        dq_out[:, c] = dq
        term = q_raw[:, c].astype(F32) * gain[:, c] * dq
        acc = term if acc is None else acc + term
    inner[...] = jnp.zeros_like(inner)
    inner[0:1, :] = lane_sums(acc)
    relative = kv3[2 * ROWS :, 0:128].astype(F32)[12:13, 0:1]
    linked = audio_linked(AUDIO_BLOCK, info[BLOCK], 3, relative)
    for h in range(heads):
        c = cols(h)
        mean, weight = audio_tile(qd[2 * ROWS :, c], kv3[0:ROWS, c], kv3[ROWS : 2 * ROWS, c], linked)
        own_out[0:4, c] = mean[8:12]
        own_out[4:8, c] = jnp.broadcast_to(weight, mean.shape)[8:12]


def key_kernel(info, xl, xc, l1, c1, l2, c2, l3, c3, stat, s1, s2, s3, k_raw, gain,
               dk_out, gv_out, inner, kv0, qd0, qd1, qd2, qd3, dv, sems):
    heads = kv0.shape[1] // HEAD_WIDTH
    even = info[EVEN] == 1
    copies = [
        Pick(even, xc, xl, kv0, sems.at[0]),
        Pick(even, xl, xc, qd0, sems.at[1]),
        Pick(even, c1, l1, qd1, sems.at[2]),
        Pick(even, c2, l2, qd2, sems.at[3]),
        Pick(even, c3, l3, qd3, sems.at[4]),
    ]
    for copy in copies:
        copy.start()
    copies[0].wait()

    def tile(qd, rows, first):
        for h in range(heads):
            c = cols(h)
            q, g, k, v = qd[0:ROWS, c], qd[ROWS : 2 * ROWS, c], kv0[0:ROWS, c], kv0[ROWS : 2 * ROWS, c]
            p = jnp.exp2(dot_nt(k, q) * SCALE2 - rows[h : h + 1, :])
            dlogit = (p * (dot_nt(v, g) - rows[16 + h : 17 + h, :])).astype(BF16)
            dk = dot_nn(dlogit, q)
            dvt = dot_nn(p.astype(BF16), g)
            dk_out[:, c] = dk if first else dk_out[:, c] + dk
            dv[:, c] = dvt if first else dv[:, c] + dvt

    copies[1].wait()
    tile(qd0, stat[...].T[0:32], True)
    for t, qd, rows in ((1, qd1, s1), (2, qd2, s2), (3, qd3, s3)):
        copies[1 + t].wait()

        @pl.when(info[AHEAD + t - 1] == 1)
        def _():
            tile(qd, rows, False)

    acc = None
    for h in range(heads):
        c = cols(h)
        dk = dk_out[:, c] * SCALE
        dk_out[:, c] = dk
        term = k_raw[:, c].astype(F32) * gain[:, c] * dk
        acc = term if acc is None else acc + term
        gv_out[:, c] = dv[:, c].astype(BF16)
    inner[...] = jnp.zeros_like(inner)
    inner[0:1, :] = lane_sums(acc)


def grad_kernel(row, raw, dn, e0, e1, i0, i1, gain, out):
    f = factors(e0, e1)[row : row + 1]
    inner = i0[0:1, :] + i1[0:1, :]
    fr = as_rows(f)
    back = as_rows(f * f * f * inner / D)
    for h in range(raw.shape[1] // HEAD_WIDTH):
        c = cols(h)
        out[:, c] = (fr * gain[:, c] * dn[:, c] - raw[:, c].astype(F32) * back).astype(BF16)


def audio_kernel(a0, a1, r1, r2, r3, info, out):
    means = [a0[0:4, :], a1[0:4, :]]
    weights = [a0[4:8, :], a1[4:8, :]]
    for d, r in enumerate((r1, r2, r3)):
        means.append(r[0:4, :])
        weights.append(jnp.where(info[AHEAD + d] == 1, r[4:8, :], MASKED))
    top = weights[0]
    for w in weights[1:]:
        top = jnp.maximum(top, w)
    mass, total = None, None
    for m, w in zip(means, weights):
        ratio = jnp.exp2(w - top)
        mass = ratio if mass is None else mass + ratio
        total = ratio * m if total is None else total + ratio * m
    out[...] = (total / mass).astype(BF16)


def on_device(
    video_query, video_key, video_value, audio_query, audio_key, audio_value,
    video_query_gain, video_key_gain, audio_query_gain, audio_key_gain,
    tile_flags, audio_centers, out_grad,
):
    blocks = lax.axis_size("ctx")
    width = video_query.shape[1]
    heads = width // HEAD_WIDTH
    block = lax.axis_index("ctx").astype(jnp.int32)

    link1 = [(i, i + 1) for i in range(1, blocks - 1, 2)] + [(i + 1, i) for i in range(1, blocks - 1, 2)]
    link2 = [(i, i + 2) for i in range(0, blocks - 2, 2)] + [(i, i - 2) for i in range(3, blocks, 2)]
    link3 = [(i, i + 3) for i in range(1, blocks - 3, 2)] + [(i, i - 3) for i in range(4, blocks, 2)]
    chip = [(i, i + 1) for i in range(0, blocks, 2)] + [(i + 1, i) for i in range(0, blocks, 2)]

    def send(x, pairs):
        return lax.ppermute(x, "ctx", pairs)

    def back(x, by):
        return send(x, [(i, i - by) for i in range(by, blocks)])

    def swap(x):
        return lax.ppermute(x, "tp", [(0, 1), (1, 0)])

    steps = jnp.arange(BACK, dtype=jnp.int32)
    info = jnp.concatenate([
        (1 - block % 2)[None],
        tile_flags[0] * (block - 1 - steps >= 0),
        block[None],
        audio_centers,
        (block + 1 + steps < blocks).astype(jnp.int32),
        jnp.full((7,), blocks * AUDIO_ROWS, jnp.int32),
    ]).astype(jnp.int32)
    relative = (audio_centers[0] - (block * AUDIO_ROWS + AUDIO_ROWS // 2)).astype(BF16)
    audio = jnp.concatenate([
        audio_key, audio_value, audio_query, jnp.full((AUDIO_ROWS, width), relative, BF16)
    ])
    gains = [g[None, :] for g in (video_query_gain, video_key_gain, audio_query_gain, audio_key_gain)]

    wide = ((ROWS, width), F32)
    tall = ((PAYLOAD, width), BF16)
    small = ((8, ROWS), F32)
    mail = ((8, width), F32)
    buffer = pltpu.VMEM((PAYLOAD, width), BF16)
    unit = 2 * heads * ROWS * ROWS * HEAD_WIDTH
    mega = ROWS * width * 4

    (energy,) = call(
        energy_kernel, [small], [VMEM] * 3, [pltpu.VMEM((128, 128), F32)], nbytes=mega, name="energy"
    )(video_query, video_key, audio)
    peer = swap(energy)
    xl, xc = call(
        prep_kernel, [tall, tall], [SMEM] + [VMEM] * 11, nbytes=3 * mega, name="prep"
    )(info, video_query, video_key, video_value, out_grad, audio, energy, peer, *gains)

    l1 = send(xl, link1)
    c1 = send(xc, chip)
    l2 = send(xc, link2)
    t3 = send(xl[2 * ROWS :], link3)
    l3 = send(l1, link2)
    c2 = send(l1, chip)
    c3 = send(l2, chip)

    stat_shape = ((ROWS, 128), F32)
    o_state, ml, cross, dqx, own_a, m1, m2, m3 = call(
        mid_kernel,
        [wide, stat_shape, wide, wide, mail, mail, mail, mail],
        [SMEM] + [ANY] * 8,
        [buffer] * 4 + [pltpu.VMEM((128, width), BF16), pltpu.SemaphoreType.DMA((11,))],
        flops=9 * unit, nbytes=8 * mega, name="mid",
    )(info, xl, xc, l1, c1, l2, c2, c3, t3)
    r1, r2, r3 = back(m1, 1), back(m2, 2), back(m3, 3)

    stats = ((32, ROWS), F32)
    video, stat, s1, s2, s3 = call(
        last_kernel,
        [((ROWS, width), BF16), stat_shape, stats, stats, stats],
        [SMEM] + [ANY] * 4 + [VMEM] * 3,
        [buffer] * 2 + [pltpu.SemaphoreType.DMA((2,))],
        flops=3 * unit, nbytes=6 * mega, name="last",
    )(info, xl, xc, l3, c3, o_state, ml, cross)
    n1, n2, n3 = back(s1, 1), back(s2, 2), back(s3, 3)

    dq, inner_q, own_b = call(
        query_kernel,
        [wide, small, mail],
        [SMEM] + [ANY] * 8 + [VMEM] * 4,
        [buffer] * 5 + [pltpu.SemaphoreType.DMA((5,))],
        flops=12 * unit, nbytes=9 * mega, name="query",
    )(info, xl, xc, l1, c1, l2, c2, l3, c3, dqx, stat, video_query, gains[0])
    peer_q = swap(inner_q)

    dk, grad_value, inner_k = call(
        key_kernel,
        [wide, ((ROWS, width), BF16), small],
        [SMEM] + [ANY] * 8 + [VMEM] * 6,
        [buffer] * 5 + [pltpu.VMEM((ROWS, width), F32), pltpu.SemaphoreType.DMA((5,))],
        flops=16 * unit, nbytes=9 * mega, name="key",
    )(info, xl, xc, l1, c1, l2, c2, l3, c3, stat, n1, n2, n3, video_key, gains[1])
    peer_k = swap(inner_k)

    def gradient(row, raw, dn, mine, other, gain, name):
        return call(
            lambda *refs: grad_kernel(row, *refs), [((ROWS, width), BF16)], [VMEM] * 7, nbytes=2 * mega, name=name
        )(raw, dn, energy, peer, mine, other, gain)[0]

    grad_query = gradient(0, video_query, dq, inner_q, peer_q, gains[0], "grad_q")
    (audio_out,) = call(
        audio_kernel, [((AUDIO_ROWS, width), BF16)], [VMEM] * 5 + [SMEM], nbytes=mega // 8, name="audio"
    )(own_a, own_b, r1, r2, r3, info)
    grad_key = gradient(1, video_key, dk, inner_k, peer_k, gains[1], "grad_k")
    return (video, audio_out, grad_query, grad_key, grad_value)


def solution(mesh):
    rows = P("ctx", "tp")
    return jax.shard_map(
        on_device,
        mesh=mesh,
        in_specs=(rows,) * 6 + (P("tp"),) * 4 + (P("ctx", None), P("ctx"), rows),
        out_specs=(rows,) * 5,
        check_vma=False,
    )
```

```python
import math

import jax
import jax.numpy as jnp
from jax import lax
from jax.experimental import pallas as pl
from jax.experimental.pallas import tpu as pltpu
from jax.sharding import PartitionSpec as P

D = 3072
HEAD_WIDTH = 128
AUD_REACH = 8
EPSILON = 1e-06
MASKED = -1e30
BACK = 3
ROWS = 256
AUDIO_ROWS = 4
SEAT = 16
SCALE = HEAD_WIDTH ** (-0.5)
SCALE2 = SCALE * math.log2(math.e)
F32 = jnp.float32
BF16 = jnp.bfloat16
VMEM_LIMIT = 20 * 1024 * 1024
LOAD_LIMIT = 63 * 1024 * 1024

EVEN, LIVE, BLOCK, CENTER, AHEAD, TOTAL_AUDIO = 0, 1, 4, 5, 6, 9

VMEM = pl.BlockSpec(memory_space=pltpu.VMEM)
SMEM = pl.BlockSpec(memory_space=pltpu.SMEM)
HBM = pl.BlockSpec(memory_space=pltpu.HBM)


def cols(head):
    return slice(head * HEAD_WIDTH, (head + 1) * HEAD_WIDTH)


def dot_nt(a, b):
    return lax.dot_general(a, b, (((1,), (1,)), ((), ())), preferred_element_type=F32)


def when_odd(even):
    return pl.when(jnp.logical_not(even))


def dot_nn(a, b):
    return lax.dot_general(a, b, (((1,), (0,)), ((), ())), preferred_element_type=F32)


def dot_tn(a, b):
    return lax.dot_general(a, b, (((0,), (0,)), ((), ())), preferred_element_type=F32)


def call(kernel, outs, ins, scratch=(), name=None, limit=VMEM_LIMIT, same=None, out_specs=None):
    return pl.pallas_call(
        kernel,
        out_shape=[jax.ShapeDtypeStruct(s, d) for s, d in outs],
        in_specs=ins,
        out_specs=out_specs or [VMEM] * len(outs),
        input_output_aliases=same or {},
        scratch_shapes=list(scratch),
        compiler_params=pltpu.CompilerParams(vmem_limit_bytes=limit),
        cost_estimate=pl.CostEstimate(flops=1, bytes_accessed=1, transcendentals=0),
        name=name,
    )


def lane_sums(wide):
    return jnp.sum(wide.T, axis=0, keepdims=True)


def as_rows(lanes):
    return jnp.broadcast_to(lanes, (HEAD_WIDTH, lanes.shape[1])).T


def first_kernel(v, g, link, sem):
    even = lax.axis_index("ctx") % 2 == 0

    @pl.when(even)
    def _():
        pltpu.make_async_copy(g, link, sem).start()

    @when_odd(even)
    def _():
        pltpu.make_async_copy(v, link, sem).start()

    pltpu.make_async_copy(g, link, sem).wait()


def join_kernel(keys, values, out):
    out[0:ROWS, :] = keys[...]
    out[ROWS:, :] = values[...]


def energy_kernel(q, k, a, energy, q_out, k_out, scr):
    heads = q.shape[1] // HEAD_WIDTH

    def squares(ref, to=None):
        total = None
        for h in range(heads):
            x = ref[:, cols(h)]
            if to is not None:
                to[:, cols(h)] = x
            x = x.astype(F32)
            total = x * x if total is None else total + x * x
        return total

    energy[...] = jnp.zeros_like(energy)
    scr[...] = jnp.zeros_like(scr)
    scr[0:SEAT, :] = squares(a)
    energy[2:3, 0:128] = lane_sums(scr[...])
    energy[0:1, :] = lane_sums(squares(q, q_out))
    energy[1:2, :] = lane_sums(squares(k, k_out))


def load_kernel(v_in, g_in, after, v, g, sems):
    del after
    copies = [pltpu.make_async_copy(v_in, v, sems.at[0]), pltpu.make_async_copy(g_in, g, sems.at[1])]
    for copy in copies:
        copy.start()
    for copy in copies:
        copy.wait()


def factors(e0, e1):
    return lax.rsqrt((e0[...] + e1[...]) / D + EPSILON)


def prep_kernel(info, q, k, v, g, a, e0, e1, gq, gk, gaq, gak, after, qn, kn, an, link, chip):
    del after
    heads = q.shape[1] // HEAD_WIDTH
    f = factors(e0, e1)
    fq, fk = as_rows(f[0:1]), as_rows(f[1:2])
    row = lax.broadcasted_iota(jnp.int32, (SEAT, 128), 0)
    is_key, is_query = row < 4, (row >= 8) & (row < 12)
    fa = jnp.where(is_key | is_query, as_rows(f[2:3, 0:128])[0:SEAT], 1.0)
    even = info[EVEN] == 1
    for h in range(heads):
        c = cols(h)
        x = (k[:, c].astype(F32) * fk * gk[:, c]).astype(BF16)
        y = (q[:, c].astype(F32) * fq * gq[:, c]).astype(BF16)
        kn[:, c] = x
        qn[:, c] = y
        ga = jnp.where(is_key, gak[:, c], jnp.where(is_query, gaq[:, c], 1.0))
        an[:, c] = (a[:, c].astype(F32) * fa * ga).astype(BF16)
        link[:, c] = jnp.where(even, y, x)
        chip[0:ROWS, c] = jnp.where(even, x, y)
        chip[ROWS:, c] = jnp.where(even, v[:, c], g[:, c])


def halves(ref):
    return ref.at[pl.ds(0, ROWS)], ref.at[pl.ds(ROWS, ROWS)]


def pick(even, first, second, c):
    return jnp.where(even, first[:, c], second[:, c])


def lead_parts(scores, dots):
    peak = scores[0]
    for s in scores[1:]:
        peak = jnp.maximum(peak, s)
    peak = jnp.max(peak, axis=0, keepdims=True) * SCALE2
    ps, mass, dot = [], None, None
    for s, dp in zip(scores, dots):
        p = jnp.exp2(s * SCALE2 - peak)
        x = p * dp
        ps.append(p)
        mass, dot = (p, x) if mass is None else (mass + p, dot + x)
    return ps, peak, jnp.sum(mass, axis=0, keepdims=True), jnp.sum(dot, axis=0, keepdims=True)


def split(x):
    return [x[i : i + ROWS] for i in range(0, x.shape[0], ROWS)]


def own_kernel(info, qn, g, kn, v, c1, part, out_t, a_t, b_t):
    c1k, c1v = halves(c1)
    heads = qn.shape[1] // HEAD_WIDTH
    live = (info[LIVE] == 1) & (info[EVEN] == 0)

    def lead(h):
        c = cols(h)
        k = jnp.concatenate([kn[:, c], c1k[:, c]])
        x = jnp.concatenate([v[:, c], c1v[:, c]])
        return k, x, dot_nt(k, qn[:, c]), dot_nt(x, g[:, c])

    for h, (k, x, s, dp) in ahead_of(list(range(heads)), lead):
        c = cols(h)
        s0, s1 = split(s)
        dots = split(dp)
        ps, peak, mass, dot = lead_parts([s0, jnp.where(live, s1, MASKED)], dots)
        share = 1.0 / mass
        mean = dot * share
        p = jnp.concatenate([y.astype(BF16) for y in ps])
        d = jnp.concatenate([(y * (z - mean)).astype(BF16) for y, z in zip(ps, dots)])
        out_t[c, :] = dot_tn(x, p) * share
        b_t[c, :] = dot_tn(k, p) * share
        a_t[c, :] = dot_tn(k, d) * share
        part[h : h + 1, :] = peak + jnp.log2(mass)
        part[heads + h : heads + h + 1, :] = mean


def next_kernel(info, qn, g, l1k, l1v, c2k, c2v, part_in, out_in, a_in, b_in, part, helper, out_t, a_t, b_t, raw):
    heads = qn.shape[1] // HEAD_WIDTH
    even = info[EVEN] == 1
    live = jnp.where(even, info[LIVE], info[LIVE + 1]) == 1

    def lead(h):
        c = cols(h)
        k, x = pick(even, l1k, c2k, c), pick(even, l1v, c2v, c)
        return k, x, dot_nt(k, qn[:, c]), dot_nt(x, g[:, c])

    for h, (k, x, s, dp) in ahead_of(list(range(heads)), lead):
        c = cols(h)
        before, mean_in = part_in[h : h + 1, :], part_in[heads + h : heads + h + 1, :]
        s = jnp.where(live, s, MASKED)
        peak = jnp.maximum(before, jnp.max(s, axis=0, keepdims=True) * SCALE2)
        p = jnp.exp2(s * SCALE2 - peak)
        decay = jnp.exp2(before - peak)
        mass = decay + jnp.sum(p, axis=0, keepdims=True)
        share = 1.0 / mass
        decay = decay * share
        mean = mean_in * decay + jnp.sum(p * dp, axis=0, keepdims=True) * share
        d = (p * (dp - mean)).astype(BF16)
        p = p.astype(BF16)
        held = b_in[c, :]
        out_t[c, :] = out_in[c, :] * decay + dot_tn(x, p) * share
        a_t[c, :] = (a_in[c, :] + (mean_in - mean) * held) * decay + dot_tn(k, d) * share
        b_t[c, :] = held * decay + dot_tn(k, p) * share
        part[h : h + 1, :] = peak + jnp.log2(mass)
        part[heads + h : heads + h + 1, :] = mean

    def lead(h):
        c = cols(h)
        return dot_nt(c2k[:, c], l1k[:, c]), dot_nt(c2v[:, c], l1v[:, c])

    @when_odd(even)
    def _():
        tile_stats(heads, lead, raw, helper)


def tile_stats(heads, lead, raw, out):
    for h, (s, dp) in ahead_of(list(range(heads)), lead):
        _, peak, mass, dot = lead_parts([s], [dp])
        raw[h : h + 1, :] = peak
        raw[16 + h : 17 + h, :] = mass
        raw[32 + h : 33 + h, :] = dot
    mass = raw[16 : 16 + heads, :]
    out[0:heads, :] = raw[0:heads, :] + jnp.log2(mass)
    out[heads : 2 * heads, :] = raw[32 : 32 + heads, :] / mass


def stat_kernel(info, qn, g, l2, c3, part, helper, m1, m2, m3, stat, s1, s2, s3, new, raw):
    l2k, l2v = halves(l2)
    c3k, c3v = halves(c3)
    heads = qn.shape[1] // HEAD_WIDTH
    even = info[EVEN] == 1
    live = jnp.where(even, info[LIVE + 1], info[LIVE + 2]) == 1
    helped = even & (info[LIVE + 2] == 1)

    def lead(h):
        c = cols(h)
        return dot_nt(pick(even, l2k, c3k, c), qn[:, c]), dot_nt(pick(even, l2v, c3v, c), g[:, c])

    tile_stats(heads, lead, raw, new)
    a, b = slice(0, heads), slice(heads, 2 * heads)
    weights = [part[a, :], jnp.where(live, new[a, :], MASKED), jnp.where(helped, helper[a, :], MASKED)]
    mean, weight = merged([part[b, :], new[b, :], jnp.where(helped, helper[b, :], 0.0)], weights)
    stat[a, :] = weight
    stat[b, :] = mean
    for s, (msg, mail) in enumerate(((s1, m1), (s2, m2), (s3, m3))):
        msg[a, :] = jnp.where(info[LIVE + s] == 0, -MASKED, weight)
        msg[b, :] = mean
        msg[2 * heads :, :] = mail[...]


def merged(means, weights):
    top = weights[0]
    for w in weights[1:]:
        top = jnp.maximum(top, w)
    mass, total = None, None
    for m, w in zip(means, weights):
        ratio = jnp.exp2(w - top)
        mass = ratio if mass is None else mass + ratio
        total = ratio * m if total is None else total + ratio * m
    return total / mass, top + jnp.log2(mass)


def side_kernel(info, qn, g, kn, v, an, mate, t1, t2, t3, u1, u2, cross, dqx, m1, m2, m3, aw):
    heads = qn.shape[1] // HEAD_WIDTH
    even = info[EVEN] == 1
    block = info[BLOCK]
    for h in range(heads):
        c = cols(h)
        own, other, x1, x2, x3, y1, y2 = (ref[:, c] for ref in (an, mate, t1, t2, t3, u1, u2))
        when_even = (x3, x2, x1, own, other, y1, y2)
        otherwise = (y2, y1, other, own, x1, x2, x3)
        for j in range(7):
            aw[SEAT * j : SEAT * (j + 1), c] = jnp.where(even, when_even[j], otherwise[j])
        aw[SEAT * 7 : SEAT * 8, c] = jnp.zeros((SEAT, HEAD_WIDTH), BF16)
    row = lax.broadcasted_iota(jnp.int32, (8 * SEAT, 1), 0)
    token = row % SEAT
    position = (block - BACK + row // SEAT) * AUDIO_ROWS + token
    linked = (
        (token < AUDIO_ROWS) & (row < 7 * SEAT) & (position >= 0) & (position < info[TOTAL_AUDIO])
        & (jnp.abs(position - info[CENTER]) <= AUD_REACH)
    )
    row = lax.broadcasted_iota(jnp.int32, (3 * SEAT, 1), 0)
    token = row % SEAT - 8
    position = (block - BACK + row // SEAT) * AUDIO_ROWS + token
    asking = (
        (token >= 0) & (token < AUDIO_ROWS) & (position >= 0)
        & (jnp.abs(position - info[CENTER]) <= AUD_REACH)
    )

    def lead(h):
        c = cols(h)
        ak = aw[:, c]
        av = pltpu.roll(ak.astype(F32), 8 * SEAT - 4, 0).astype(BF16)
        return ak, av, dot_nt(ak, qn[:, c]), dot_nt(av, g[:, c]), dot_nt(ak[0 : 3 * SEAT], kn[:, c])

    ahead = lead(0)
    for h in range(heads):
        c = cols(h)
        ak, av, s, dp, x = ahead
        if h + 1 < heads:
            ahead = lead(h + 1)
        s = jnp.where(linked, s, MASKED)
        p = jnp.exp2((s - jnp.max(s, axis=0, keepdims=True)) * SCALE2)
        share = p * (1.0 / jnp.sum(p, axis=0, keepdims=True))
        rounded = share.astype(BF16)
        cross[c, :] = dot_tn(av, rounded)
        row_dot = jnp.sum(rounded.astype(F32) * dp, axis=0, keepdims=True)
        dqx[c, :] = dot_tn(ak, (share * (dp - row_dot)).astype(BF16))
        x = x * SCALE2
        peak = jnp.max(x, axis=1, keepdims=True)
        w = jnp.exp2(x - peak)
        mass = jnp.sum(w, axis=1, keepdims=True)
        mean = dot_nn(w.astype(BF16), v[:, c]) / mass
        weight = jnp.where(asking, peak + jnp.log2(mass), MASKED)
        half = slice((h % 2) * HEAD_WIDTH, (h % 2 + 1) * HEAD_WIDTH)
        for msg, j in ((m3, 0), (m2, 1), (m1, 2)):
            for i in range(AUDIO_ROWS):
                r, to = SEAT * j + 8 + i, i * (heads // 2) + h // 2
                msg[to : to + 1, half] = mean[r : r + 1]
            r = SEAT * j + 8
            msg[2 * heads : 2 * heads + AUDIO_ROWS, h : h + 1] = weight[r : r + AUDIO_ROWS]


def attend(lse, delta, s, dp):
    p = jnp.exp2(s * SCALE2 - lse)
    return p.astype(BF16), (p * (dp - delta)).astype(BF16)


def ahead_of(items, lead):
    ready = lead(items[0])
    for n, item in enumerate(items):
        now = ready
        if n + 1 < len(items):
            ready = lead(items[n + 1])
        yield item, now


def finish_queries(h, out, dq, cross, dqx, q_raw, gain, video, dn, total):
    c = cols(h)
    video[:, c] = (out + cross[c, :]).T.astype(BF16)
    d = ((dq + dqx[c, :]) * SCALE).T
    dn[:, c] = d
    term = q_raw[:, c].astype(F32) * gain[:, c] * d
    return term if total is None else total + term


def main_kernel(info, qn, g, kn, v, part, stat, out_p, a_p, b_p, l2, c3, cross, dqx, q_raw, gain,
                out_t, dq_t, dk, dv, video, dq, inner):
    l2k, l2v = halves(l2)
    c3k, c3v = halves(c3)
    heads = qn.shape[1] // HEAD_WIDTH
    even = info[EVEN] == 1
    live = jnp.where(even, info[LIVE + 1], info[LIVE + 2]) == 1

    def lead(h):
        c = cols(h)
        k = jnp.concatenate([pick(even, l2k, c3k, c), kn[:, c]])
        x = jnp.concatenate([pick(even, l2v, c3v, c), v[:, c]])
        return k[0:ROWS], x[0:ROWS], dot_nt(k, qn[:, c]), dot_nt(x, g[:, c])

    for h, (k, x, s, dp) in ahead_of(list(range(heads)), lead):
        c = cols(h)
        lse, delta = stat[h : h + 1, :], stat[heads + h : heads + h + 1, :]
        p, dlogit = attend(jnp.where(live, lse, -MASKED), delta, s[0:ROWS], dp[0:ROWS])
        own_p, own_dlogit = attend(lse, delta, s[ROWS:], dp[ROWS:])
        decay = jnp.exp2(part[h : h + 1, :] - lse)
        shift = part[heads + h : heads + h + 1, :] - delta
        out_t[c, :] = out_p[c, :] * decay + dot_tn(x, p)
        dq_t[c, :] = (a_p[c, :] + shift * b_p[c, :]) * decay + dot_tn(k, dlogit)
        dk[:, c] = dot_nn(own_dlogit, qn[:, c])
        dv[:, c] = dot_nn(own_p, g[:, c])
    inner[...] = jnp.zeros_like(inner)

    @when_odd(even)
    def _():
        total = None
        for h in range(heads):
            c = cols(h)
            total = finish_queries(h, out_t[c, :], dq_t[c, :], cross, dqx, q_raw, gain, video, dq, total)
        inner[0:1, :] = lane_sums(total)


def finish_keys(h, dk, dv, k_raw, gain, gv, dn, total):
    c = cols(h)
    d = dk * SCALE
    dn[:, c] = d
    gv[:, c] = dv.astype(BF16)
    term = k_raw[:, c].astype(F32) * gain[:, c] * d
    return term if total is None else total + term


def key_kernel(info, kn, v, n1, n2, n3, l1k, l1v, c1, l2, c2k, c2v, c3, dk_in, dv_in, k_raw, gain, inner_q,
               dk_out, dv_out, gv, inner):
    c1k, c1v = halves(c1)
    l2k, l2v = halves(l2)
    c3k, c3v = halves(c3)
    heads = kn.shape[1] // HEAD_WIDTH
    even = info[EVEN] == 1
    queries = ((c1k, l1k), (c2k, l2k))
    grads = ((c1v, l1v), (c2v, l2v))
    stats = (None, n1, n2)
    items = [(h, t) for h in range(heads) for t in range(1, BACK)]

    def lead(item):
        h, t = item
        c = cols(h)
        q, o = pick(even, *queries[t - 1], c), pick(even, *grads[t - 1], c)
        return q, o, dot_nt(kn[:, c], q), dot_nt(v[:, c], o)

    for (h, t), (q, o, s, dp) in ahead_of(items, lead):
        c = cols(h)
        lse = jnp.where(info[AHEAD + t - 1] == 1, stats[t][h : h + 1, :], -MASKED)
        p, dlogit = attend(lse, stats[t][heads + h : heads + h + 1, :], s, dp)
        x, y = dot_nn(dlogit, q), dot_nn(p, o)
        dk, dv = (dk_in[:, c] + x, dv_in[:, c] + y) if t == 1 else (dk + x, dv + y)
        if t == BACK - 1:
            dk_out[:, cols(h)] = dk
            dv_out[:, cols(h)] = dv
    inner[...] = inner_q[...]

    @pl.when(even)
    def _():
        def lead(h):
            c = cols(h)
            return dot_nt(kn[:, c], c3k[:, c]), dot_nt(v[:, c], c3v[:, c])

        total = None
        for h, (s, dp) in ahead_of(list(range(heads)), lead):
            c = cols(h)
            lse = jnp.where(info[AHEAD + 2] == 1, n3[h : h + 1, :], -MASKED)
            p, dlogit = attend(lse, n3[heads + h : heads + h + 1, :], s, dp)
            dk = dk_out[:, c] + dot_nn(dlogit, c3k[:, c])
            dv = dv_out[:, c] + dot_nn(p, c3v[:, c])
            total = finish_keys(h, dk, dv, k_raw, gain, gv, dk_out, total)
        inner[0:1, :] = lane_sums(total)


def final_kernel(info, qn, g, kn, v, stat, n3, l3, out_t, dq_t, dk_in, dv_in, cross, dqx, video_in, gv_in,
                 q_raw, k_raw, gq, gk, video, gv, dn, inner):
    del video_in, gv_in
    l3k, l3v = halves(l3)
    heads = qn.shape[1] // HEAD_WIDTH
    even = info[EVEN] == 1
    inner[...] = jnp.zeros_like(inner)
    every = list(range(heads))

    @pl.when(even)
    def _():
        def lead(h):
            c = cols(h)
            return dot_nt(l3k[:, c], qn[:, c]), dot_nt(l3v[:, c], g[:, c])

        total = None
        for h, (s, dp) in ahead_of(every, lead):
            c = cols(h)
            lse = jnp.where(info[LIVE + 2] == 1, stat[h : h + 1, :], -MASKED)
            p, dlogit = attend(lse, stat[heads + h : heads + h + 1, :], s, dp)
            out = out_t[c, :] + dot_tn(l3v[:, c], p)
            dq = dq_t[c, :] + dot_tn(l3k[:, c], dlogit)
            total = finish_queries(h, out, dq, cross, dqx, q_raw, gq, video, dn, total)
        inner[0:1, :] = lane_sums(total)

    @when_odd(even)
    def _():
        def lead(h):
            c = cols(h)
            return dot_nt(kn[:, c], l3k[:, c]), dot_nt(v[:, c], l3v[:, c])

        total = None
        for h, (s, dp) in ahead_of(every, lead):
            c = cols(h)
            lse = jnp.where(info[AHEAD + 2] == 1, n3[h : h + 1, :], -MASKED)
            p, dlogit = attend(lse, n3[heads + h : heads + h + 1, :], s, dp)
            dk = dk_in[:, c] + dot_nn(dlogit, l3k[:, c])
            dv = dv_in[:, c] + dot_nn(p, l3v[:, c])
            total = finish_keys(h, dk, dv, k_raw, gk, gv, dn, total)
        inner[0:1, :] = lane_sums(total)


def norm_back(row, raw, gain, dn, e0, e1, i0, i1, out, part=None):
    f = factors(e0, e1)[row : row + 1]
    inner = i0[0:1, :] + i1[0:1, :]
    fr = as_rows(f)
    back = as_rows(f * f * f * inner / D)
    heads = raw.shape[1] // HEAD_WIDTH
    for h in range(heads) if part is None else range(part * heads // 2, (part + 1) * heads // 2):
        c = cols(h)
        out[:, c] = (fr * gain[:, c] * dn[:, c] - raw[:, c].astype(F32) * back).astype(BF16)


def late_kernel(info, q, k, gq, gk, dn, e0, e1, i0, i1, gq_in, gk_in, grad_q, grad_k, held, sems):
    del gq_in, gk_in
    even = info[EVEN] == 1
    half = held.shape[1] // 2

    def fill(row, raw, gain, out):
        for i in range(2):
            c = pl.ds(i * half, half)
            norm_back(row, raw, gain, dn, e0, e1, i0, i1, held, i)
            pltpu.make_async_copy(held.at[:, c], out.at[:, c], sems.at[i]).start()

    @pl.when(even)
    def _():
        fill(0, q, gq, grad_q)

    @when_odd(even)
    def _():
        fill(1, k, gk, grad_k)

    for i in range(2):
        c = pl.ds(i * half, half)
        pltpu.make_async_copy(held.at[:, c], grad_q.at[:, c], sems.at[i]).wait()


def shadow_kernel(info, kn, v, an, mate, t1, t2, t3, u1, u2,
                  l1k, l1v, c1, l2, c2k, c2v, l3, c3, r1, r2, r3,
                  q, k, gq, gk, dq, dk, e0, e1, i0, i1, video_in, gv_in,
                  out, video, gv, grad_q, grad_k, held, grad, sems):
    c1k, c1v = halves(c1)
    l2k, l2v = halves(l2)
    l3k, l3v = halves(l3)
    c3k, c3v = halves(c3)
    heads = kn.shape[1] // HEAD_WIDTH
    even, block = info[EVEN] == 1, info[BLOCK]
    pltpu.make_async_copy(video_in, video, sems.at[0]).start()
    pltpu.make_async_copy(gv_in, gv, sems.at[1]).start()

    @pl.when(even)
    def _():
        norm_back(1, k, gk, dk, e0, e1, i0, i1, grad)
        pltpu.make_async_copy(grad, grad_k, sems.at[2]).start()

    @when_odd(even)
    def _():
        norm_back(0, q, gq, dq, e0, e1, i0, i1, grad)
        pltpu.make_async_copy(grad, grad_q, sems.at[2]).start()

    keys = ((l1k, c1k), (l2k, c2k), (l3k, c3k))
    values = ((l1v, c1v), (l2v, c2v), (l3v, c3v))
    token = lax.broadcasted_iota(jnp.int32, (SEAT, 1), 0) - 8
    asks = (token >= 0) & (token < AUDIO_ROWS)
    linked = [asks & (jnp.abs(block * AUDIO_ROWS + token - info[CENTER]) <= AUD_REACH)]
    c = cols(0)
    for t, (first, second) in enumerate(((t1, mate), (t2, u1), (t3, u2))):
        seat = jnp.where(even, first[:, c], second[:, c]).astype(F32)
        gap = (token + AUDIO_ROWS * (t + 1) - 2).astype(F32) - seat[12:13, 0:1]
        linked.append(asks & (block - t - 1 >= 0) & (jnp.abs(gap) <= AUD_REACH))

    def lead(h):
        c = cols(h)
        k = jnp.concatenate([kn[:, c]] + [pick(even, *pair, c) for pair in keys])
        x = dot_nt(an[:, c], k) * SCALE2
        return [jnp.where(m, x[:, t * ROWS : (t + 1) * ROWS], MASKED) for t, m in enumerate(linked)]

    for h, found in ahead_of(list(range(heads)), lead):
        c = cols(h)
        peak = jnp.maximum(jnp.maximum(found[0], found[1]), jnp.maximum(found[2], found[3]))
        peak = jnp.max(peak, axis=1, keepdims=True)
        ws = [jnp.exp2(x - peak) for x in found]
        mass = jnp.sum((ws[0] + ws[1]) + (ws[2] + ws[3]), axis=1, keepdims=True)
        w = jnp.concatenate([x.astype(BF16) for x in ws], axis=1)
        x = jnp.concatenate([v[:, c]] + [pick(even, *pair, c) for pair in values])
        held[0:SEAT, c] = dot_nn(w, x) / mass
        held[SEAT : 2 * SEAT, c] = jnp.broadcast_to(peak + jnp.log2(mass), (SEAT, HEAD_WIDTH))
    for d, r in enumerate((r1, r2, r3)):
        base = 2 * SEAT + SEAT * d
        for i in range(AUDIO_ROWS):
            for j in range(heads // 2):
                at = 2 * heads + i * (heads // 2) + j
                held[base + i : base + i + 1, 2 * j * HEAD_WIDTH : 2 * (j + 1) * HEAD_WIDTH] = r[at : at + 1, :]
        w = jnp.where(info[AHEAD + d] == 1, r[4 * heads : 4 * heads + 8, 0:HEAD_WIDTH], MASKED)
        for h in range(heads):
            held[base + 8 : base + SEAT, cols(h)] = jnp.broadcast_to(w[:, h : h + 1], (8, HEAD_WIDTH))
    for h in range(heads):
        c = cols(h)
        means, weights = [held[8:12, c]], [held[SEAT + 8 : SEAT + 12, c]]
        for d in range(BACK):
            base = 2 * SEAT + SEAT * d
            means.append(held[base : base + 4, c])
            weights.append(held[base + 8 : base + 12, c])
        out[:, c] = merged(means, weights)[0].astype(BF16)
    pltpu.make_async_copy(video_in, video, sems.at[0]).wait()
    pltpu.make_async_copy(gv_in, gv, sems.at[1]).wait()
    pltpu.make_async_copy(grad, grad_q, sems.at[2]).wait()


def on_device(
    video_query, video_key, video_value, audio_query, audio_key, audio_value,
    video_query_gain, video_key_gain, audio_query_gain, audio_key_gain,
    tile_flags, audio_centers, out_grad,
):
    blocks = lax.axis_size("ctx")
    width = video_query.shape[1]
    heads = width // HEAD_WIDTH
    block = lax.axis_index("ctx").astype(jnp.int32)

    link1 = [(i, i + 1) for i in range(1, blocks - 1, 2)] + [(i + 1, i) for i in range(1, blocks - 1, 2)]
    link2 = [(i, i + 2) for i in range(0, blocks - 2, 2)] + [(i, i - 2) for i in range(3, blocks, 2)]
    link3 = [(i, i + 3) for i in range(1, blocks - 3, 2)] + [(i, i - 3) for i in range(4, blocks, 2)]
    chip = [(i, i + 1) for i in range(0, blocks, 2)] + [(i + 1, i) for i in range(0, blocks, 2)]
    forward = [(i, i + 1) for i in range(1, blocks - 1, 2)]

    def send(x, pairs):
        return lax.ppermute(x, "ctx", pairs)

    def back(x, by):
        return send(x, [(i, i - by) for i in range(by, blocks)])

    def swap(x):
        return lax.ppermute(x, "tp", [(0, 1), (1, 0)])

    steps = jnp.arange(BACK, dtype=jnp.int32)
    info = jnp.concatenate([
        (1 - block % 2)[None],
        tile_flags[0] * (block - 1 - steps >= 0),
        block[None],
        audio_centers,
        (block + 1 + steps < blocks).astype(jnp.int32),
        jnp.full((7,), blocks * AUDIO_ROWS, jnp.int32),
    ]).astype(jnp.int32)
    relative = (audio_centers[0] - (block * AUDIO_ROWS + AUDIO_ROWS // 2)).astype(BF16)
    audio = jnp.concatenate([
        audio_key, audio_value, audio_query, jnp.full((AUDIO_ROWS, width), relative, BF16)
    ])
    gq, gk, gaq, gak = (g[None, :] for g in (video_query_gain, video_key_gain, audio_query_gain, audio_key_gain))

    full = ((ROWS, width), BF16)
    wide = ((ROWS, width), F32)
    turned = ((width, ROWS), F32)
    pair = ((2 * ROWS, width), BF16)
    small = ((8, ROWS), F32)
    mail = ((2 * heads + 8, ROWS), F32)
    stats = ((2 * heads, ROWS), F32)
    letter = ((4 * heads + 8, ROWS), F32)

    def after(x, *done):
        return lax.optimization_barrier((x, *done))[0]

    (xv,) = call(
        first_kernel, [full], [HBM, HBM], [pltpu.SemaphoreType.DMA(())], name="first", limit=LOAD_LIMIT
    )(video_value, out_grad)
    l1v = send(xv, link1)

    energy, q, k = call(
        energy_kernel, [small, full, full], [VMEM] * 3, [pltpu.VMEM((128, 128), F32)], name="energy"
    )(video_query, video_key, audio)
    peer = swap(energy)
    v, g = call(
        load_kernel, [full, full], [HBM, HBM, VMEM], [pltpu.SemaphoreType.DMA((2,))], name="load"
    )(video_value, out_grad, energy)
    qn, kn, an, xk, both = call(
        prep_kernel, [full, full, ((SEAT, width), BF16), full, pair], [SMEM] + [VMEM] * 11 + [HBM], name="prep",
    )(info, q, k, v, g, audio, energy, peer, gq, gk, gaq, gak, l1v)

    l1k, c1, c2v = send(xk, link1), send(both, chip), send(l1v, chip)
    mate, t1, t2, t3 = send(an, chip), send(an, link1), send(an, link2), send(an, link3)
    part, out_p, a_p, b_p = call(
        own_kernel, [stats, turned, turned, turned], [SMEM] + [VMEM] * 5, name="own",
    )(info, qn, g, kn, v, c1)
    c2k = send(l1k, chip)
    l2 = send(after(both, l1k, t1, t2, t3, part), link2)
    u1, u2 = send(t1, chip), send(t2, chip)
    (l1,) = call(join_kernel, [pair], [VMEM] * 2, name="join")(l1k, l1v)
    part, helper, out_p, a_p, b_p = call(
        next_kernel, [stats, stats, turned, turned, turned], [SMEM] + [VMEM] * 10, [pltpu.VMEM((48, ROWS), F32)],
        name="next", same={8: 2, 9: 3, 10: 4},
    )(info, qn, g, l1k, l1v, c2k, c2v, part, out_p, a_p, b_p)
    helped = send(helper, forward)
    cross, dqx, m1, m2, m3 = call(
        side_kernel,
        [turned, turned, mail, mail, mail],
        [SMEM] + [VMEM] * 11, [pltpu.VMEM((8 * SEAT, width), BF16)], name="side",
    )(info, qn, g, kn, v, an, mate, t1, t2, t3, u1, u2)
    l2, l1, _, _, _ = lax.optimization_barrier((l2, l1, part, m1, helped))
    c3 = send(l2, chip)
    l3 = send(l1, link2)
    stat, s1, s2, s3 = call(
        stat_kernel, [stats, letter, letter, letter], [SMEM] + [VMEM] * 9,
        [pltpu.VMEM((2 * heads, ROWS), F32), pltpu.VMEM((48, ROWS), F32)],
        name="stat",
    )(info, qn, g, l2, c3, part, helped, m1, m2, m3)
    n1, n2, n3 = back(s1, 1), back(s2, 2), back(s3, 3)

    out_t, dq_t, dk, dv, video, dq, inner_q = call(
        main_kernel, [turned, turned, wide, wide, full, wide, small], [SMEM] + [VMEM] * 15,
        name="main",
    )(info, qn, g, kn, v, part, stat, out_p, a_p, b_p, l2, c3, cross, dqx, q, gq)
    dk, dv, value, inner = call(
        key_kernel, [wide, wide, full, small], [SMEM] + [VMEM] * 17,
        name="key", same={13: 0, 14: 1},
    )(info, kn, v, n1, n2, n3, l1k, l1v, c1, l2, c2k, c2v, c3, dk, dv, k, gk, inner_q)
    inner_peer = swap(inner)
    video, value, dn, last = call(
        final_kernel, [full, full, wide, small], [SMEM] + [VMEM] * 19,
        name="final", same={14: 0, 15: 1},
    )(info, qn, g, kn, v, stat, n3, l3, out_t, dq_t, dk, dv, cross, dqx, video, value, q, k, gq, gk)
    last_peer = swap(last)
    audio_out, video, value, grad_query, grad_key = call(
        shadow_kernel, [((AUDIO_ROWS, width), BF16)] + [full] * 4, [SMEM] + [VMEM] * 32,
        [
            pltpu.VMEM((5 * SEAT, width), F32), pltpu.VMEM((ROWS, width), BF16),
            pltpu.SemaphoreType.DMA((3,)),
        ],
        name="shadow", out_specs=[VMEM] + [HBM] * 4,
    )(
        info, kn, v, an, mate, t1, t2, t3, u1, u2,
        l1k, l1v, c1, l2, c2k, c2v, l3, c3, n1, n2, n3,
        q, k, gq, gk, dq, dk, energy, peer, inner, inner_peer, video, value,
    )
    grad_query, grad_key = call(
        late_kernel, [full, full], [SMEM] + [VMEM] * 9 + [HBM] * 2,
        [pltpu.VMEM((ROWS, width), BF16), pltpu.SemaphoreType.DMA((2,))],
        name="late", same={10: 0, 11: 1}, out_specs=[HBM] * 2,
    )(info, q, k, gq, gk, dn, energy, peer, last, last_peer, grad_query, grad_key)
    return (video, audio_out, grad_query, grad_key, value)


def solution(mesh):
    rows = P("ctx", "tp")
    return jax.shard_map(
        on_device,
        mesh=mesh,
        in_specs=(rows,) * 6 + (P("tp"),) * 4 + (P("ctx", None), P("ctx"), rows),
        out_specs=(rows,) * 5,
        check_vma=False,
    )
```

```python
import math

import jax
import jax.numpy as jnp
from jax import lax
from jax.experimental import pallas as pl
from jax.experimental.pallas import tpu as pltpu
from jax.sharding import PartitionSpec as P

D = 3072
HEAD_WIDTH = 128
AUD_REACH = 8
EPSILON = 1e-06
MASKED = -1e30
BACK = 3
ROWS = 256
AUDIO_ROWS = 4
SEAT = 16
SCALE = HEAD_WIDTH ** (-0.5)
SCALE2 = SCALE * math.log2(math.e)
F32 = jnp.float32
BF16 = jnp.bfloat16
VMEM_LIMIT = 20 * 1024 * 1024
LOAD_LIMIT = 63 * 1024 * 1024

EVEN, LIVE, BLOCK, CENTER, AHEAD, TOTAL_AUDIO = 0, 1, 4, 5, 6, 9

VMEM = pl.BlockSpec(memory_space=pltpu.VMEM)
SMEM = pl.BlockSpec(memory_space=pltpu.SMEM)
HBM = pl.BlockSpec(memory_space=pltpu.HBM)


def cols(head):
    return slice(head * HEAD_WIDTH, (head + 1) * HEAD_WIDTH)


def dot_nt(a, b):
    return lax.dot_general(a, b, (((1,), (1,)), ((), ())), preferred_element_type=F32)


def when_odd(even):
    return pl.when(jnp.logical_not(even))


def dot_nn(a, b):
    return lax.dot_general(a, b, (((1,), (0,)), ((), ())), preferred_element_type=F32)


def dot_tn(a, b):
    return lax.dot_general(a, b, (((0,), (0,)), ((), ())), preferred_element_type=F32)


def call(kernel, outs, ins, scratch=(), name=None, limit=VMEM_LIMIT, same=None, out_specs=None):
    return pl.pallas_call(
        kernel,
        out_shape=[jax.ShapeDtypeStruct(s, d) for s, d in outs],
        in_specs=ins,
        out_specs=out_specs or [VMEM] * len(outs),
        input_output_aliases=same or {},
        scratch_shapes=list(scratch),
        compiler_params=pltpu.CompilerParams(vmem_limit_bytes=limit),
        cost_estimate=pl.CostEstimate(flops=1, bytes_accessed=1, transcendentals=0),
        name=name,
    )


def lane_sums(wide):
    return jnp.sum(wide.T, axis=0, keepdims=True)


def as_rows(lanes):
    return jnp.broadcast_to(lanes, (HEAD_WIDTH, lanes.shape[1])).T


def first_kernel(v, g, link, sem):
    even = lax.axis_index("ctx") % 2 == 0

    @pl.when(even)
    def _():
        pltpu.make_async_copy(g, link, sem).start()

    @when_odd(even)
    def _():
        pltpu.make_async_copy(v, link, sem).start()

    pltpu.make_async_copy(g, link, sem).wait()


def strip_kernel(tall, out):
    out[...] = tall[0:ROWS, :]


def seats_of(l1k, c2k, t3):
    first, second = pl.ds(ROWS, SEAT), pl.ds(ROWS + SEAT, SEAT)
    return l1k.at[first], l1k.at[second], t3, c2k.at[first], c2k.at[second]


def energy_kernel(q, k, a, mate, energy, q_out, k_out, scr):
    heads = q.shape[1] // HEAD_WIDTH

    def squares(ref, to=None):
        total = None
        for h in range(heads):
            x = ref[:, cols(h)]
            if to is not None:
                to[:, cols(h)] = x
            x = x.astype(F32)
            total = x * x if total is None else total + x * x
        return total

    energy[...] = jnp.zeros_like(energy)
    scr[...] = jnp.zeros_like(scr)
    scr[0:SEAT, :] = squares(a)
    scr[SEAT : 2 * SEAT, :] = squares(mate)
    energy[2:3, 0:128] = lane_sums(scr[...])
    energy[0:1, :] = lane_sums(squares(q, q_out))
    energy[1:2, :] = lane_sums(squares(k, k_out))


def load_kernel(v_in, g_in, after, v, g, sems):
    del after
    copies = [pltpu.make_async_copy(v_in, v, sems.at[0]), pltpu.make_async_copy(g_in, g, sems.at[1])]
    for copy in copies:
        copy.start()
    for copy in copies:
        copy.wait()


def factors(e0, e1):
    return lax.rsqrt((e0[...] + e1[...]) / D + EPSILON)


def prep_kernel(info, q, k, v, g, a, mate, e0, e1, gq, gk, gaq, gak, l1v, qn, kn, an, mn, link, chip):
    del l1v
    heads = q.shape[1] // HEAD_WIDTH
    f = factors(e0, e1)
    fq, fk = as_rows(f[0:1]), as_rows(f[1:2])
    row = lax.broadcasted_iota(jnp.int32, (SEAT, 128), 0)
    is_key, is_query = row < 4, (row >= 8) & (row < 12)
    fa = as_rows(f[2:3, 0:128])
    even = info[EVEN] == 1
    for h in range(heads):
        c = cols(h)
        x = (k[:, c].astype(F32) * fk * gk[:, c]).astype(BF16)
        y = (q[:, c].astype(F32) * fq * gq[:, c]).astype(BF16)
        kn[:, c] = x
        qn[:, c] = y
        link[0:ROWS, c] = jnp.where(even, y, x)
        chip[0:ROWS, c] = jnp.where(even, x, y)
        chip[ROWS:, c] = jnp.where(even, v[:, c], g[:, c])
        gain = jnp.where(is_key, gak[:, c], jnp.where(is_query, gaq[:, c], 1.0))
        for i, (raw, out) in enumerate(((a, an), (mate, mn))):
            norm = jnp.where(is_key | is_query, fa[SEAT * i : SEAT * (i + 1)], 1.0)
            audio = (raw[:, c].astype(F32) * norm * gain).astype(BF16)
            out[:, c] = audio
            link[ROWS + SEAT * i : ROWS + SEAT * (i + 1), c] = audio


def top(ref):
    return ref.at[pl.ds(0, ROWS)]


def halves(ref):
    return ref.at[pl.ds(0, ROWS)], ref.at[pl.ds(ROWS, ROWS)]


def pick(even, first, second, c):
    return jnp.where(even, first[:, c], second[:, c])


def lead_parts(scores, dots):
    peak = scores[0]
    for s in scores[1:]:
        peak = jnp.maximum(peak, s)
    peak = jnp.max(peak, axis=0, keepdims=True) * SCALE2
    ps, mass, dot = [], None, None
    for s, dp in zip(scores, dots):
        p = jnp.exp2(s * SCALE2 - peak)
        x = p * dp
        ps.append(p)
        mass, dot = (p, x) if mass is None else (mass + p, dot + x)
    return ps, peak, jnp.sum(mass, axis=0, keepdims=True), jnp.sum(dot, axis=0, keepdims=True)


def split(x):
    return [x[i : i + ROWS] for i in range(0, x.shape[0], ROWS)]


def own_kernel(info, qn, g, kn, v, c1, c2v, part, out_t, a_t, b_t):
    del c2v
    c1k, c1v = halves(c1)
    heads = qn.shape[1] // HEAD_WIDTH
    live = (info[LIVE] == 1) & (info[EVEN] == 0)

    def lead(h):
        c = cols(h)
        k = jnp.concatenate([kn[:, c], c1k[:, c]])
        x = jnp.concatenate([v[:, c], c1v[:, c]])
        return k, x, dot_nt(k, qn[:, c]), dot_nt(x, g[:, c])

    for h, (k, x, s, dp) in ahead_of(list(range(heads)), lead):
        c = cols(h)
        s0, s1 = split(s)
        dots = split(dp)
        ps, peak, mass, dot = lead_parts([s0, jnp.where(live, s1, MASKED)], dots)
        share = 1.0 / mass
        mean = dot * share
        p = jnp.concatenate([y.astype(BF16) for y in ps])
        d = jnp.concatenate([(y * (z - mean)).astype(BF16) for y, z in zip(ps, dots)])
        out_t[c, :] = dot_tn(x, p) * share
        b_t[c, :] = dot_tn(k, p) * share
        a_t[c, :] = dot_tn(k, d) * share
        part[h : h + 1, :] = peak + jnp.log2(mass)
        part[heads + h : heads + h + 1, :] = mean


def next_kernel(info, qn, g, l1k, l1v, c2k, c2v, part_in, out_in, a_in, b_in, part, helper, out_t, a_t, b_t, raw):
    l1k, c2k = top(l1k), top(c2k)
    heads = qn.shape[1] // HEAD_WIDTH
    even = info[EVEN] == 1
    live = jnp.where(even, info[LIVE], info[LIVE + 1]) == 1

    def lead(h):
        c = cols(h)
        k, x = pick(even, l1k, c2k, c), pick(even, l1v, c2v, c)
        return k, x, dot_nt(k, qn[:, c]), dot_nt(x, g[:, c])

    for h, (k, x, s, dp) in ahead_of(list(range(heads)), lead):
        c = cols(h)
        before, mean_in = part_in[h : h + 1, :], part_in[heads + h : heads + h + 1, :]
        s = jnp.where(live, s, MASKED)
        peak = jnp.maximum(before, jnp.max(s, axis=0, keepdims=True) * SCALE2)
        p = jnp.exp2(s * SCALE2 - peak)
        decay = jnp.exp2(before - peak)
        mass = decay + jnp.sum(p, axis=0, keepdims=True)
        share = 1.0 / mass
        decay = decay * share
        mean = mean_in * decay + jnp.sum(p * dp, axis=0, keepdims=True) * share
        d = (p * (dp - mean)).astype(BF16)
        p = p.astype(BF16)
        held = b_in[c, :]
        out_t[c, :] = out_in[c, :] * decay + dot_tn(x, p) * share
        a_t[c, :] = (a_in[c, :] + (mean_in - mean) * held) * decay + dot_tn(k, d) * share
        b_t[c, :] = held * decay + dot_tn(k, p) * share
        part[h : h + 1, :] = peak + jnp.log2(mass)
        part[heads + h : heads + h + 1, :] = mean

    def lead(h):
        c = cols(h)
        return dot_nt(c2k[:, c], l1k[:, c]), dot_nt(c2v[:, c], l1v[:, c])

    @when_odd(even)
    def _():
        tile_stats(heads, lead, raw, helper)


def tile_stats(heads, lead, raw, out):
    for h, (s, dp) in ahead_of(list(range(heads)), lead):
        _, peak, mass, dot = lead_parts([s], [dp])
        raw[h : h + 1, :] = peak
        raw[16 + h : 17 + h, :] = mass
        raw[32 + h : 33 + h, :] = dot
    mass = raw[16 : 16 + heads, :]
    out[0:heads, :] = raw[0:heads, :] + jnp.log2(mass)
    out[heads : 2 * heads, :] = raw[32 : 32 + heads, :] / mass


def stat_kernel(info, qn, g, l2, c3, part, helper, m1, m2, m3, stat, s1, s2, s3, new, raw):
    l2k, l2v = halves(l2)
    c3k, c3v = halves(c3)
    heads = qn.shape[1] // HEAD_WIDTH
    even = info[EVEN] == 1
    live = jnp.where(even, info[LIVE + 1], info[LIVE + 2]) == 1
    helped = even & (info[LIVE + 2] == 1)

    def lead(h):
        c = cols(h)
        return dot_nt(pick(even, l2k, c3k, c), qn[:, c]), dot_nt(pick(even, l2v, c3v, c), g[:, c])

    tile_stats(heads, lead, raw, new)
    a, b = slice(0, heads), slice(heads, 2 * heads)
    weights = [part[a, :], jnp.where(live, new[a, :], MASKED), jnp.where(helped, helper[a, :], MASKED)]
    mean, weight = merged([part[b, :], new[b, :], jnp.where(helped, helper[b, :], 0.0)], weights)
    stat[a, :] = weight
    stat[b, :] = mean
    for s, (msg, mail) in enumerate(((s1, m1), (s2, m2), (s3, m3))):
        msg[a, :] = jnp.where(info[LIVE + s] == 0, -MASKED, weight)
        msg[b, :] = mean
        msg[2 * heads :, :] = mail[...]


def merged(means, weights):
    peak = weights[0]
    for w in weights[1:]:
        peak = jnp.maximum(peak, w)
    mass, total = None, None
    for m, w in zip(means, weights):
        ratio = jnp.exp2(w - peak)
        mass = ratio if mass is None else mass + ratio
        total = ratio * m if total is None else total + ratio * m
    return total / mass, peak + jnp.log2(mass)


def side_kernel(info, qn, g, kn, v, an, mate, l1k, c2k, t3, cross, dqx, m1, m2, m3, aw):
    heads = qn.shape[1] // HEAD_WIDTH
    even = info[EVEN] == 1
    block = info[BLOCK]
    refs = (an, mate, *seats_of(l1k, c2k, t3))
    for h in range(heads):
        c = cols(h)
        own, other, x1, x2, x3, y1, y2 = (ref[:, c] for ref in refs)
        when_even = (x3, x2, x1, own, other, y1, y2)
        otherwise = (y2, y1, other, own, x1, x2, x3)
        for j in range(7):
            aw[SEAT * j : SEAT * (j + 1), c] = jnp.where(even, when_even[j], otherwise[j])
        aw[SEAT * 7 : SEAT * 8, c] = jnp.zeros((SEAT, HEAD_WIDTH), BF16)
    row = lax.broadcasted_iota(jnp.int32, (8 * SEAT, 1), 0)
    token = row % SEAT
    position = (block - BACK + row // SEAT) * AUDIO_ROWS + token
    linked = (
        (token < AUDIO_ROWS) & (row < 7 * SEAT) & (position >= 0) & (position < info[TOTAL_AUDIO])
        & (jnp.abs(position - info[CENTER]) <= AUD_REACH)
    )
    row = lax.broadcasted_iota(jnp.int32, (3 * SEAT, 1), 0)
    token = row % SEAT - 8
    position = (block - BACK + row // SEAT) * AUDIO_ROWS + token
    asking = (
        (token >= 0) & (token < AUDIO_ROWS) & (position >= 0)
        & (jnp.abs(position - info[CENTER]) <= AUD_REACH)
    )

    def lead(h):
        c = cols(h)
        ak = aw[:, c]
        av = pltpu.roll(ak.astype(F32), 8 * SEAT - 4, 0).astype(BF16)
        return ak, av, dot_nt(ak, qn[:, c]), dot_nt(av, g[:, c]), dot_nt(ak[0 : 3 * SEAT], kn[:, c])

    ahead = lead(0)
    for h in range(heads):
        c = cols(h)
        ak, av, s, dp, x = ahead
        if h + 1 < heads:
            ahead = lead(h + 1)
        s = jnp.where(linked, s, MASKED)
        p = jnp.exp2((s - jnp.max(s, axis=0, keepdims=True)) * SCALE2)
        share = p * (1.0 / jnp.sum(p, axis=0, keepdims=True))
        rounded = share.astype(BF16)
        cross[c, :] = dot_tn(av, rounded)
        row_dot = jnp.sum(rounded.astype(F32) * dp, axis=0, keepdims=True)
        dqx[c, :] = dot_tn(ak, (share * (dp - row_dot)).astype(BF16))
        x = x * SCALE2
        peak = jnp.max(x, axis=1, keepdims=True)
        w = jnp.exp2(x - peak)
        mass = jnp.sum(w, axis=1, keepdims=True)
        mean = dot_nn(w.astype(BF16), v[:, c]) / mass
        weight = jnp.where(asking, peak + jnp.log2(mass), MASKED)
        half = slice((h % 2) * HEAD_WIDTH, (h % 2 + 1) * HEAD_WIDTH)
        for msg, j in ((m3, 0), (m2, 1), (m1, 2)):
            for i in range(AUDIO_ROWS):
                r, to = SEAT * j + 8 + i, i * (heads // 2) + h // 2
                msg[to : to + 1, half] = mean[r : r + 1]
            r = SEAT * j + 8
            msg[2 * heads : 2 * heads + AUDIO_ROWS, h : h + 1] = weight[r : r + AUDIO_ROWS]


def attend(lse, delta, s, dp):
    p = jnp.exp2(s * SCALE2 - lse)
    return p.astype(BF16), (p * (dp - delta)).astype(BF16)


def ahead_of(items, lead):
    ready = lead(items[0])
    for n, item in enumerate(items):
        now = ready
        if n + 1 < len(items):
            ready = lead(items[n + 1])
        yield item, now


def finish_queries(h, out, dq, cross, dqx, q_raw, gain, video, dn, total):
    c = cols(h)
    video[:, c] = (out + cross[c, :]).T.astype(BF16)
    d = ((dq + dqx[c, :]) * SCALE).T
    dn[:, c] = d
    term = q_raw[:, c].astype(F32) * gain[:, c] * d
    return term if total is None else total + term


def main_kernel(info, qn, g, kn, v, part, stat, out_p, a_p, b_p, l2, c3, cross, dqx, q_raw, gain, l3v,
                out_t, dq_t, dk, dv, video, dq, inner):
    del l3v
    l2k, l2v = halves(l2)
    c3k, c3v = halves(c3)
    heads = qn.shape[1] // HEAD_WIDTH
    even = info[EVEN] == 1
    live = jnp.where(even, info[LIVE + 1], info[LIVE + 2]) == 1

    def lead(h):
        c = cols(h)
        k = jnp.concatenate([pick(even, l2k, c3k, c), kn[:, c]])
        x = jnp.concatenate([pick(even, l2v, c3v, c), v[:, c]])
        return k[0:ROWS], x[0:ROWS], dot_nt(k, qn[:, c]), dot_nt(x, g[:, c])

    for h, (k, x, s, dp) in ahead_of(list(range(heads)), lead):
        c = cols(h)
        lse, delta = stat[h : h + 1, :], stat[heads + h : heads + h + 1, :]
        p, dlogit = attend(jnp.where(live, lse, -MASKED), delta, s[0:ROWS], dp[0:ROWS])
        own_p, own_dlogit = attend(lse, delta, s[ROWS:], dp[ROWS:])
        decay = jnp.exp2(part[h : h + 1, :] - lse)
        shift = part[heads + h : heads + h + 1, :] - delta
        out_t[c, :] = out_p[c, :] * decay + dot_tn(x, p)
        dq_t[c, :] = (a_p[c, :] + shift * b_p[c, :]) * decay + dot_tn(k, dlogit)
        dk[:, c] = dot_nn(own_dlogit, qn[:, c])
        dv[:, c] = dot_nn(own_p, g[:, c])
    inner[...] = jnp.zeros_like(inner)

    @when_odd(even)
    def _():
        total = None
        for h in range(heads):
            c = cols(h)
            total = finish_queries(h, out_t[c, :], dq_t[c, :], cross, dqx, q_raw, gain, video, dq, total)
        inner[0:1, :] = lane_sums(total)


def finish_keys(h, dk, dv, k_raw, gain, gv, dn, total):
    c = cols(h)
    d = dk * SCALE
    dn[:, c] = d
    gv[:, c] = dv.astype(BF16)
    term = k_raw[:, c].astype(F32) * gain[:, c] * d
    return term if total is None else total + term


def key_kernel(info, kn, v, n1, n2, n3, l1k, l1v, c1, l2, c2k, c2v, c3, dk_in, dv_in, k_raw, gain, inner_q, video_in,
               dk_out, dv_out, gv, inner, video, sem):
    c1k, c1v = halves(c1)
    l2k, l2v = halves(l2)
    c3k, c3v = halves(c3)
    heads = kn.shape[1] // HEAD_WIDTH
    even = info[EVEN] == 1

    @when_odd(even)
    def _():
        pltpu.make_async_copy(video_in, video, sem).start()

    l1k, c2k = top(l1k), top(c2k)
    queries = ((c1k, l1k), (c2k, l2k))
    grads = ((c1v, l1v), (c2v, l2v))
    stats = (None, n1, n2)
    items = [(h, t) for h in range(heads) for t in range(1, BACK)]

    def lead(item):
        h, t = item
        c = cols(h)
        q, o = pick(even, *queries[t - 1], c), pick(even, *grads[t - 1], c)
        return q, o, dot_nt(kn[:, c], q), dot_nt(v[:, c], o)

    for (h, t), (q, o, s, dp) in ahead_of(items, lead):
        c = cols(h)
        lse = jnp.where(info[AHEAD + t - 1] == 1, stats[t][h : h + 1, :], -MASKED)
        p, dlogit = attend(lse, stats[t][heads + h : heads + h + 1, :], s, dp)
        x, y = dot_nn(dlogit, q), dot_nn(p, o)
        dk, dv = (dk_in[:, c] + x, dv_in[:, c] + y) if t == 1 else (dk + x, dv + y)
        if t == BACK - 1:
            dk_out[:, cols(h)] = dk
            dv_out[:, cols(h)] = dv
    inner[...] = inner_q[...]

    @pl.when(even)
    def _():
        def lead(h):
            c = cols(h)
            return dot_nt(kn[:, c], c3k[:, c]), dot_nt(v[:, c], c3v[:, c])

        total = None
        for h, (s, dp) in ahead_of(list(range(heads)), lead):
            c = cols(h)
            lse = jnp.where(info[AHEAD + 2] == 1, n3[h : h + 1, :], -MASKED)
            p, dlogit = attend(lse, n3[heads + h : heads + h + 1, :], s, dp)
            dk = dk_out[:, c] + dot_nn(dlogit, c3k[:, c])
            dv = dv_out[:, c] + dot_nn(p, c3v[:, c])
            total = finish_keys(h, dk, dv, k_raw, gain, gv, dk_out, total)
        inner[0:1, :] = lane_sums(total)

    @when_odd(even)
    def _():
        pltpu.make_async_copy(video_in, video, sem).wait()


def final_kernel(info, qn, g, kn, v, stat, n3, l3k, l3v, out_t, dq_t, dk_in, dv_in, cross, dqx, gv_in,
                 q_raw, k_raw, gq, gk, result, gv, dn, inner, sem):
    heads = qn.shape[1] // HEAD_WIDTH
    even = info[EVEN] == 1

    @pl.when(even)
    def _():
        pltpu.make_async_copy(gv_in, gv, sem).start()

    inner[...] = jnp.zeros_like(inner)
    every = list(range(heads))

    @pl.when(even)
    def _():
        def lead(h):
            c = cols(h)
            return dot_nt(l3k[:, c], qn[:, c]), dot_nt(l3v[:, c], g[:, c])

        total = None
        for h, (s, dp) in ahead_of(every, lead):
            c = cols(h)
            lse = jnp.where(info[LIVE + 2] == 1, stat[h : h + 1, :], -MASKED)
            p, dlogit = attend(lse, stat[heads + h : heads + h + 1, :], s, dp)
            out = out_t[c, :] + dot_tn(l3v[:, c], p)
            dq = dq_t[c, :] + dot_tn(l3k[:, c], dlogit)
            total = finish_queries(h, out, dq, cross, dqx, q_raw, gq, result, dn, total)
        inner[0:1, :] = lane_sums(total)

    @when_odd(even)
    def _():
        def lead(h):
            c = cols(h)
            return dot_nt(kn[:, c], l3k[:, c]), dot_nt(v[:, c], l3v[:, c])

        total = None
        for h, (s, dp) in ahead_of(every, lead):
            c = cols(h)
            lse = jnp.where(info[AHEAD + 2] == 1, n3[h : h + 1, :], -MASKED)
            p, dlogit = attend(lse, n3[heads + h : heads + h + 1, :], s, dp)
            dk = dk_in[:, c] + dot_nn(dlogit, l3k[:, c])
            dv = dv_in[:, c] + dot_nn(p, l3v[:, c])
            total = finish_keys(h, dk, dv, k_raw, gk, result, dn, total)
        inner[0:1, :] = lane_sums(total)

    @pl.when(even)
    def _():
        pltpu.make_async_copy(gv_in, gv, sem).wait()


def norm_back(row, raw, gain, dn, e0, e1, i0, i1, out, part=None):
    f = factors(e0, e1)[row : row + 1]
    inner = i0[0:1, :] + i1[0:1, :]
    fr = as_rows(f)
    back = as_rows(f * f * f * inner / D)
    heads = raw.shape[1] // HEAD_WIDTH
    for h in range(heads) if part is None else range(part * heads // 2, (part + 1) * heads // 2):
        c = cols(h)
        out[:, c] = (fr * gain[:, c] * dn[:, c] - raw[:, c].astype(F32) * back).astype(BF16)


def late_kernel(info, q, k, gq, gk, dn, e0, e1, i0, i1, gq_in, gk_in, grad_q, grad_k, held, sems):
    del gq_in, gk_in
    even = info[EVEN] == 1
    half = held.shape[1] // 2

    def fill(row, raw, gain, out):
        for i in range(2):
            c = pl.ds(i * half, half)
            norm_back(row, raw, gain, dn, e0, e1, i0, i1, held, i)
            pltpu.make_async_copy(held.at[:, c], out.at[:, c], sems.at[i]).start()

    @pl.when(even)
    def _():
        fill(0, q, gq, grad_q)

    @when_odd(even)
    def _():
        fill(1, k, gk, grad_k)

    for i in range(2):
        c = pl.ds(i * half, half)
        pltpu.make_async_copy(held.at[:, c], grad_q.at[:, c], sems.at[i]).wait()


def shadow_kernel(info, kn, v, an, mate, t3, l1k, l1v, c1, l2, c2k, c2v, l3k, l3v, c3, r1, r2, r3,
                  q, k, gq, gk, dq, dk, e0, e1, i0, i1, result, video_in, gv_in,
                  out, video, gv, grad_q, grad_k, held, grad, sems):
    c1k, c1v = halves(c1)
    l2k, l2v = halves(l2)
    t1, t2, t3, u1, u2 = seats_of(l1k, c2k, t3)
    l1k, c2k = top(l1k), top(c2k)
    c3k, c3v = halves(c3)
    heads = kn.shape[1] // HEAD_WIDTH
    even, block = info[EVEN] == 1, info[BLOCK]
    del video_in, gv_in

    @pl.when(even)
    def _():
        pltpu.make_async_copy(result, video, sems.at[0]).start()
        norm_back(1, k, gk, dk, e0, e1, i0, i1, grad)
        pltpu.make_async_copy(grad, grad_k, sems.at[1]).start()

    @when_odd(even)
    def _():
        pltpu.make_async_copy(result, gv, sems.at[0]).start()
        norm_back(0, q, gq, dq, e0, e1, i0, i1, grad)
        pltpu.make_async_copy(grad, grad_q, sems.at[1]).start()

    keys = ((l1k, c1k), (l2k, c2k), (l3k, c3k))
    values = ((l1v, c1v), (l2v, c2v), (l3v, c3v))
    token = lax.broadcasted_iota(jnp.int32, (SEAT, 1), 0) - 8
    asks = (token >= 0) & (token < AUDIO_ROWS)
    linked = [asks & (jnp.abs(block * AUDIO_ROWS + token - info[CENTER]) <= AUD_REACH)]
    c = cols(0)
    for t, (first, second) in enumerate(((t1, mate), (t2, u1), (t3, u2))):
        seat = jnp.where(even, first[:, c], second[:, c]).astype(F32)
        gap = (token + AUDIO_ROWS * (t + 1) - 2).astype(F32) - seat[12:13, 0:1]
        linked.append(asks & (block - t - 1 >= 0) & (jnp.abs(gap) <= AUD_REACH))

    def lead(h):
        c = cols(h)
        k = jnp.concatenate([kn[:, c]] + [pick(even, *pair, c) for pair in keys])
        x = dot_nt(an[:, c], k) * SCALE2
        return [jnp.where(m, x[:, t * ROWS : (t + 1) * ROWS], MASKED) for t, m in enumerate(linked)]

    for h, found in ahead_of(list(range(heads)), lead):
        c = cols(h)
        peak = jnp.maximum(jnp.maximum(found[0], found[1]), jnp.maximum(found[2], found[3]))
        peak = jnp.max(peak, axis=1, keepdims=True)
        ws = [jnp.exp2(x - peak) for x in found]
        mass = jnp.sum((ws[0] + ws[1]) + (ws[2] + ws[3]), axis=1, keepdims=True)
        w = jnp.concatenate([x.astype(BF16) for x in ws], axis=1)
        x = jnp.concatenate([v[:, c]] + [pick(even, *pair, c) for pair in values])
        held[0:SEAT, c] = dot_nn(w, x) / mass
        held[SEAT : 2 * SEAT, c] = jnp.broadcast_to(peak + jnp.log2(mass), (SEAT, HEAD_WIDTH))
    for d, r in enumerate((r1, r2, r3)):
        base = 2 * SEAT + SEAT * d
        for i in range(AUDIO_ROWS):
            for j in range(heads // 2):
                at = 2 * heads + i * (heads // 2) + j
                held[base + i : base + i + 1, 2 * j * HEAD_WIDTH : 2 * (j + 1) * HEAD_WIDTH] = r[at : at + 1, :]
        w = jnp.where(info[AHEAD + d] == 1, r[4 * heads : 4 * heads + 8, 0:HEAD_WIDTH], MASKED)
        for h in range(heads):
            held[base + 8 : base + SEAT, cols(h)] = jnp.broadcast_to(w[:, h : h + 1], (8, HEAD_WIDTH))
    for h in range(heads):
        c = cols(h)
        means, weights = [held[8:12, c]], [held[SEAT + 8 : SEAT + 12, c]]
        for d in range(BACK):
            base = 2 * SEAT + SEAT * d
            means.append(held[base : base + 4, c])
            weights.append(held[base + 8 : base + 12, c])
        out[:, c] = merged(means, weights)[0].astype(BF16)
    pltpu.make_async_copy(result, video, sems.at[0]).wait()
    pltpu.make_async_copy(grad, grad_q, sems.at[1]).wait()


def on_device(
    video_query, video_key, video_value, audio_query, audio_key, audio_value,
    video_query_gain, video_key_gain, audio_query_gain, audio_key_gain,
    tile_flags, audio_centers, out_grad,
):
    blocks = lax.axis_size("ctx")
    width = video_query.shape[1]
    heads = width // HEAD_WIDTH
    block = lax.axis_index("ctx").astype(jnp.int32)

    link1 = [(i, i + 1) for i in range(1, blocks - 1, 2)] + [(i + 1, i) for i in range(1, blocks - 1, 2)]
    link2 = [(i, i + 2) for i in range(0, blocks - 2, 2)] + [(i, i - 2) for i in range(3, blocks, 2)]
    link3 = [(i, i + 3) for i in range(1, blocks - 3, 2)] + [(i, i - 3) for i in range(4, blocks, 2)]
    chip = [(i, i + 1) for i in range(0, blocks, 2)] + [(i + 1, i) for i in range(0, blocks, 2)]
    forward = [(i, i + 1) for i in range(1, blocks - 1, 2)]

    def send(x, pairs):
        return lax.ppermute(x, "ctx", pairs)

    def back(x, by):
        return send(x, [(i, i - by) for i in range(by, blocks)])

    def swap(x):
        return lax.ppermute(x, "tp", [(0, 1), (1, 0)])

    steps = jnp.arange(BACK, dtype=jnp.int32)
    info = jnp.concatenate([
        (1 - block % 2)[None],
        tile_flags[0] * (block - 1 - steps >= 0),
        block[None],
        audio_centers,
        (block + 1 + steps < blocks).astype(jnp.int32),
        jnp.full((7,), blocks * AUDIO_ROWS, jnp.int32),
    ]).astype(jnp.int32)
    relative = (audio_centers[0] - (block * AUDIO_ROWS + AUDIO_ROWS // 2)).astype(BF16)
    audio = jnp.concatenate([
        audio_key, audio_value, audio_query, jnp.full((AUDIO_ROWS, width), relative, BF16)
    ])
    gq, gk, gaq, gak = (g[None, :] for g in (video_query_gain, video_key_gain, audio_query_gain, audio_key_gain))

    full = ((ROWS, width), BF16)
    wide = ((ROWS, width), F32)
    turned = ((width, ROWS), F32)
    pair = ((2 * ROWS, width), BF16)
    small = ((8, ROWS), F32)
    mail = ((2 * heads + 8, ROWS), F32)
    stats = ((2 * heads, ROWS), F32)
    letter = ((4 * heads + 8, ROWS), F32)

    def after(x, *done):
        return lax.optimization_barrier((x, *done))[0]

    (xv,) = call(
        first_kernel, [full], [HBM, HBM], [pltpu.SemaphoreType.DMA(())], name="first", limit=LOAD_LIMIT
    )(video_value, out_grad)
    l1v = send(xv, link1)
    mate = send(audio, chip)

    energy, q, k = call(
        energy_kernel, [small, full, full], [VMEM] * 4, [pltpu.VMEM((128, 128), F32)], name="energy"
    )(video_query, video_key, audio, mate)
    peer = swap(energy)
    v, g = call(
        load_kernel, [full, full], [HBM, HBM, VMEM], [pltpu.SemaphoreType.DMA((2,))], name="load"
    )(video_value, out_grad, energy)
    seat = ((SEAT, width), BF16)
    qn, kn, an, mate, xk, both = call(
        prep_kernel, [full, full, seat, seat, ((ROWS + 2 * SEAT, width), BF16), pair],
        [SMEM] + [VMEM] * 12 + [HBM], name="prep",
    )(info, q, k, v, g, audio, mate, energy, peer, gq, gk, gaq, gak, l1v)

    l1k, c1, c2v = send(xk, link1), send(both, chip), send(l1v, chip)
    t3 = send(an, link3)
    l2 = send(after(both, c1), link2)
    part, out_p, a_p, b_p = call(
        own_kernel, [stats, turned, turned, turned], [SMEM] + [VMEM] * 5 + [HBM], name="own",
    )(info, qn, g, kn, v, c1, c2v)
    l1k, _ = lax.optimization_barrier((l1k, part))
    c2k = send(l1k, chip)
    (lk,) = call(strip_kernel, [full], [VMEM], name="strip")(l1k)
    part, helper, out_p, a_p, b_p = call(
        next_kernel, [stats, stats, turned, turned, turned], [SMEM] + [VMEM] * 10, [pltpu.VMEM((48, ROWS), F32)],
        name="next", same={8: 2, 9: 3, 10: 4},
    )(info, qn, g, l1k, l1v, c2k, c2v, part, out_p, a_p, b_p)
    helped = send(helper, forward)
    cross, dqx, m1, m2, m3 = call(
        side_kernel,
        [turned, turned, mail, mail, mail],
        [SMEM] + [VMEM] * 9, [pltpu.VMEM((8 * SEAT, width), BF16)], name="side",
    )(info, qn, g, kn, v, an, mate, l1k, c2k, t3)
    l2, lk, lv, _, _, _ = lax.optimization_barrier((l2, lk, l1v, part, m1, helped))
    c3 = send(l2, chip)
    l3v = send(lv, link2)
    stat, s1, s2, s3 = call(
        stat_kernel, [stats, letter, letter, letter], [SMEM] + [VMEM] * 9,
        [pltpu.VMEM((2 * heads, ROWS), F32), pltpu.VMEM((48, ROWS), F32)],
        name="stat",
    )(info, qn, g, l2, c3, part, helped, m1, m2, m3)
    n1, n2, n3 = back(s1, 1), back(s2, 2), back(s3, 3)
    l3k = send(after(lk, l3v, n1, n2, n3), link2)

    out_t, dq_t, dk, dv, video, dq, inner_q = call(
        main_kernel, [turned, turned, wide, wide, full, wide, small], [SMEM] + [VMEM] * 15 + [HBM],
        name="main",
    )(info, qn, g, kn, v, part, stat, out_p, a_p, b_p, l2, c3, cross, dqx, q, gq, l3v)
    dk, dv, value, inner, video = call(
        key_kernel, [wide, wide, full, small, full], [SMEM] + [VMEM] * 18, [pltpu.SemaphoreType.DMA(())],
        name="key", same={13: 0, 14: 1}, out_specs=[VMEM] * 4 + [HBM],
    )(info, kn, v, n1, n2, n3, l1k, l1v, c1, l2, c2k, c2v, c3, dk, dv, k, gk, inner_q, video)
    inner_peer = swap(inner)
    result, value, dn, last = call(
        final_kernel, [full, full, wide, small], [SMEM] + [VMEM] * 19, [pltpu.SemaphoreType.DMA(())],
        name="final", out_specs=[VMEM, HBM, VMEM, VMEM],
    )(info, qn, g, kn, v, stat, n3, l3k, l3v, out_t, dq_t, dk, dv, cross, dqx, value, q, k, gq, gk)
    last_peer = swap(last)
    audio_out, video, value, grad_query, grad_key = call(
        shadow_kernel, [((AUDIO_ROWS, width), BF16)] + [full] * 4, [SMEM] + [VMEM] * 28 + [HBM] * 2,
        [
            pltpu.VMEM((5 * SEAT, width), F32), pltpu.VMEM((ROWS, width), BF16),
            pltpu.SemaphoreType.DMA((2,)),
        ],
        name="shadow", out_specs=[VMEM] + [HBM] * 4, same={29: 1, 30: 2},
    )(
        info, kn, v, an, mate, t3, l1k, l1v, c1, l2, c2k, c2v, l3k, l3v, c3, n1, n2, n3,
        q, k, gq, gk, dq, dk, energy, peer, inner, inner_peer, result, video, value,
    )
    grad_query, grad_key = call(
        late_kernel, [full, full], [SMEM] + [VMEM] * 9 + [HBM] * 2,
        [pltpu.VMEM((ROWS, width), BF16), pltpu.SemaphoreType.DMA((2,))],
        name="late", same={10: 0, 11: 1}, out_specs=[HBM] * 2,
    )(info, q, k, gq, gk, dn, energy, peer, last, last_peer, grad_query, grad_key)
    return (video, audio_out, grad_query, grad_key, value)


def solution(mesh):
    rows = P("ctx", "tp")
    return jax.shard_map(
        on_device,
        mesh=mesh,
        in_specs=(rows,) * 6 + (P("tp"),) * 4 + (P("ctx", None), P("ctx"), rows),
        out_specs=(rows,) * 5,
        check_vma=False,
    )
```

```python
import math

import jax
import jax.numpy as jnp
from jax import lax
from jax.experimental import pallas as pl
from jax.experimental.pallas import tpu as pltpu
from jax.sharding import PartitionSpec as P

D = 3072
HEAD_WIDTH = 128
AUD_REACH = 8
EPSILON = 1e-06
MASKED = -1e30
BACK = 3
ROWS = 256
AUDIO_ROWS = 4
SEAT = 16
SCALE = HEAD_WIDTH ** (-0.5)
SCALE2 = SCALE * math.log2(math.e)
F32 = jnp.float32
BF16 = jnp.bfloat16
VMEM_LIMIT = 20 * 1024 * 1024
LOAD_LIMIT = 63 * 1024 * 1024

EVEN, LIVE, BLOCK, CENTER, AHEAD, TOTAL_AUDIO = 0, 1, 4, 5, 6, 9

VMEM = pl.BlockSpec(memory_space=pltpu.VMEM)
SMEM = pl.BlockSpec(memory_space=pltpu.SMEM)
HBM = pl.BlockSpec(memory_space=pltpu.HBM)


def cols(head):
    return slice(head * HEAD_WIDTH, (head + 1) * HEAD_WIDTH)


def dot_nt(a, b):
    return lax.dot_general(a, b, (((1,), (1,)), ((), ())), preferred_element_type=F32)


def when_odd(even):
    return pl.when(jnp.logical_not(even))


def dot_nn(a, b):
    return lax.dot_general(a, b, (((1,), (0,)), ((), ())), preferred_element_type=F32)


def dot_tn(a, b):
    return lax.dot_general(a, b, (((0,), (0,)), ((), ())), preferred_element_type=F32)


def call(kernel, outs, ins, scratch=(), name=None, limit=VMEM_LIMIT, same=None, out_specs=None):
    return pl.pallas_call(
        kernel,
        out_shape=[jax.ShapeDtypeStruct(s, d) for s, d in outs],
        in_specs=ins,
        out_specs=out_specs or [VMEM] * len(outs),
        input_output_aliases=same or {},
        scratch_shapes=list(scratch),
        compiler_params=pltpu.CompilerParams(vmem_limit_bytes=limit),
        cost_estimate=pl.CostEstimate(flops=1, bytes_accessed=1, transcendentals=0),
        name=name,
    )


def lane_sums(wide):
    return jnp.sum(wide.T, axis=0, keepdims=True)


def as_rows(lanes):
    return jnp.broadcast_to(lanes, (HEAD_WIDTH, lanes.shape[1])).T


def first_kernel(v, g, link, sem):
    even = lax.axis_index("ctx") % 2 == 0

    @pl.when(even)
    def _():
        pltpu.make_async_copy(g, link, sem).start()

    @when_odd(even)
    def _():
        pltpu.make_async_copy(v, link, sem).start()

    pltpu.make_async_copy(g, link, sem).wait()


def strip_kernel(tall, out):
    out[...] = tall[0:ROWS, :]


def seats_of(l1k, c2k, t3):
    first, second = pl.ds(ROWS, SEAT), pl.ds(ROWS + SEAT, SEAT)
    return l1k.at[first], l1k.at[second], t3, c2k.at[first], c2k.at[second]


def energy_kernel(q, k, a, mate, energy, q_out, k_out, scr):
    heads = q.shape[1] // HEAD_WIDTH

    def squares(ref, to=None):
        total = None
        for h in range(heads):
            x = ref[:, cols(h)]
            if to is not None:
                to[:, cols(h)] = x
            x = x.astype(F32)
            total = x * x if total is None else total + x * x
        return total

    energy[...] = jnp.zeros_like(energy)
    scr[...] = jnp.zeros_like(scr)
    scr[0:SEAT, :] = squares(a)
    scr[SEAT : 2 * SEAT, :] = squares(mate)
    energy[2:3, 0:128] = lane_sums(scr[...])
    energy[0:1, :] = lane_sums(squares(q, q_out))
    energy[1:2, :] = lane_sums(squares(k, k_out))


def load_kernel(v_in, g_in, after, v, g, sems):
    del after
    copies = [pltpu.make_async_copy(v_in, v, sems.at[0]), pltpu.make_async_copy(g_in, g, sems.at[1])]
    for copy in copies:
        copy.start()
    for copy in copies:
        copy.wait()


def factors(e0, e1):
    return lax.rsqrt((e0[...] + e1[...]) / D + EPSILON)


def prep_kernel(info, q, k, v, g, a, mate, e0, e1, gq, gk, gaq, gak, l1v, qn, kn, an, mn, link, chip):
    del l1v
    heads = q.shape[1] // HEAD_WIDTH
    f = factors(e0, e1)
    fq, fk = as_rows(f[0:1]), as_rows(f[1:2])
    row = lax.broadcasted_iota(jnp.int32, (SEAT, 128), 0)
    is_key, is_query = row < 4, (row >= 8) & (row < 12)
    fa = as_rows(f[2:3, 0:128])
    even = info[EVEN] == 1
    for h in range(heads):
        c = cols(h)
        x = (k[:, c].astype(F32) * fk * gk[:, c]).astype(BF16)
        y = (q[:, c].astype(F32) * fq * gq[:, c]).astype(BF16)
        kn[:, c] = x
        qn[:, c] = y
        link[0:ROWS, c] = jnp.where(even, y, x)
        chip[0:ROWS, c] = jnp.where(even, x, y)
        chip[ROWS:, c] = jnp.where(even, v[:, c], g[:, c])
        gain = jnp.where(is_key, gak[:, c], jnp.where(is_query, gaq[:, c], 1.0))
        for i, (raw, out) in enumerate(((a, an), (mate, mn))):
            norm = jnp.where(is_key | is_query, fa[SEAT * i : SEAT * (i + 1)], 1.0)
            audio = (raw[:, c].astype(F32) * norm * gain).astype(BF16)
            out[:, c] = audio
            link[ROWS + SEAT * i : ROWS + SEAT * (i + 1), c] = audio


def top(ref):
    return ref.at[pl.ds(0, ROWS)]


def halves(ref):
    return ref.at[pl.ds(0, ROWS)], ref.at[pl.ds(ROWS, ROWS)]


def pick(even, first, second, c):
    return jnp.where(even, first[:, c], second[:, c])


def lead_parts(scores, dots):
    peak = scores[0]
    for s in scores[1:]:
        peak = jnp.maximum(peak, s)
    peak = jnp.max(peak, axis=0, keepdims=True) * SCALE2
    ps, mass, dot = [], None, None
    for s, dp in zip(scores, dots):
        p = jnp.exp2(s * SCALE2 - peak)
        x = p * dp
        ps.append(p)
        mass, dot = (p, x) if mass is None else (mass + p, dot + x)
    return ps, peak, jnp.sum(mass, axis=0, keepdims=True), jnp.sum(dot, axis=0, keepdims=True)


def split(x):
    return [x[i : i + ROWS] for i in range(0, x.shape[0], ROWS)]


def own_kernel(info, qn, g, kn, v, c1, c2v, part, out_t, a_t, b_t):
    del c2v
    c1k, c1v = halves(c1)
    heads = qn.shape[1] // HEAD_WIDTH
    live = (info[LIVE] == 1) & (info[EVEN] == 0)

    def lead(h):
        c = cols(h)
        k = jnp.concatenate([kn[:, c], c1k[:, c]])
        x = jnp.concatenate([v[:, c], c1v[:, c]])
        return k, x, dot_nt(k, qn[:, c]), dot_nt(x, g[:, c])

    for h, (k, x, s, dp) in ahead_of(list(range(heads)), lead):
        c = cols(h)
        s0, s1 = split(s)
        dots = split(dp)
        ps, peak, mass, dot = lead_parts([s0, jnp.where(live, s1, MASKED)], dots)
        share = 1.0 / mass
        mean = dot * share
        p = jnp.concatenate([y.astype(BF16) for y in ps])
        d = jnp.concatenate([(y * (z - mean)).astype(BF16) for y, z in zip(ps, dots)])
        out_t[c, :] = dot_tn(x, p) * share
        b_t[c, :] = dot_tn(k, p) * share
        a_t[c, :] = dot_tn(k, d) * share
        part[h : h + 1, :] = peak + jnp.log2(mass)
        part[heads + h : heads + h + 1, :] = mean


def next_kernel(info, qn, g, l1k, l1v, c2k, c2v, part_in, out_in, a_in, b_in, part, helper, out_t, a_t, b_t, raw):
    l1k, c2k = top(l1k), top(c2k)
    heads = qn.shape[1] // HEAD_WIDTH
    even = info[EVEN] == 1
    live = jnp.where(even, info[LIVE], info[LIVE + 1]) == 1

    def lead(h):
        c = cols(h)
        k, x = pick(even, l1k, c2k, c), pick(even, l1v, c2v, c)
        return k, x, dot_nt(k, qn[:, c]), dot_nt(x, g[:, c])

    for h, (k, x, s, dp) in ahead_of(list(range(heads)), lead):
        c = cols(h)
        before, mean_in = part_in[h : h + 1, :], part_in[heads + h : heads + h + 1, :]
        s = jnp.where(live, s, MASKED)
        peak = jnp.maximum(before, jnp.max(s, axis=0, keepdims=True) * SCALE2)
        p = jnp.exp2(s * SCALE2 - peak)
        decay = jnp.exp2(before - peak)
        mass = decay + jnp.sum(p, axis=0, keepdims=True)
        share = 1.0 / mass
        decay = decay * share
        mean = mean_in * decay + jnp.sum(p * dp, axis=0, keepdims=True) * share
        d = (p * (dp - mean)).astype(BF16)
        p = p.astype(BF16)
        held = b_in[c, :]
        out_t[c, :] = out_in[c, :] * decay + dot_tn(x, p) * share
        a_t[c, :] = (a_in[c, :] + (mean_in - mean) * held) * decay + dot_tn(k, d) * share
        b_t[c, :] = held * decay + dot_tn(k, p) * share
        part[h : h + 1, :] = peak + jnp.log2(mass)
        part[heads + h : heads + h + 1, :] = mean

    def lead(h):
        c = cols(h)
        return dot_nt(c2k[:, c], l1k[:, c]), dot_nt(c2v[:, c], l1v[:, c])

    @when_odd(even)
    def _():
        tile_stats(heads, lead, raw, helper)


def tile_stats(heads, lead, raw, out):
    for h, (s, dp) in ahead_of(list(range(heads)), lead):
        _, peak, mass, dot = lead_parts([s], [dp])
        raw[h : h + 1, :] = peak
        raw[16 + h : 17 + h, :] = mass
        raw[32 + h : 33 + h, :] = dot
    mass = raw[16 : 16 + heads, :]
    out[0:heads, :] = raw[0:heads, :] + jnp.log2(mass)
    out[heads : 2 * heads, :] = raw[32 : 32 + heads, :] / mass


def stat_kernel(info, qn, g, l2, c3, part, helper, m1, m2, m3, stat, s1, s2, s3, new, raw):
    l2k, l2v = halves(l2)
    c3k, c3v = halves(c3)
    heads = qn.shape[1] // HEAD_WIDTH
    even = info[EVEN] == 1
    live = jnp.where(even, info[LIVE + 1], info[LIVE + 2]) == 1
    helped = even & (info[LIVE + 2] == 1)

    def lead(h):
        c = cols(h)
        return dot_nt(pick(even, l2k, c3k, c), qn[:, c]), dot_nt(pick(even, l2v, c3v, c), g[:, c])

    tile_stats(heads, lead, raw, new)
    a, b = slice(0, heads), slice(heads, 2 * heads)
    weights = [part[a, :], jnp.where(live, new[a, :], MASKED), jnp.where(helped, helper[a, :], MASKED)]
    mean, weight = merged([part[b, :], new[b, :], jnp.where(helped, helper[b, :], 0.0)], weights)
    stat[a, :] = weight
    stat[b, :] = mean
    for s, (msg, mail) in enumerate(((s1, m1), (s2, m2), (s3, m3))):
        msg[a, :] = jnp.where(info[LIVE + s] == 0, -MASKED, weight)
        msg[b, :] = mean
        msg[2 * heads :, :] = mail[...]


def merged(means, weights):
    peak = weights[0]
    for w in weights[1:]:
        peak = jnp.maximum(peak, w)
    mass, total = None, None
    for m, w in zip(means, weights):
        ratio = jnp.exp2(w - peak)
        mass = ratio if mass is None else mass + ratio
        total = ratio * m if total is None else total + ratio * m
    return total / mass, peak + jnp.log2(mass)


def mail_kernel(info, kn, v, mate, l1k, c2k, t3, l2, m1, m2, m3):
    del l2
    heads = kn.shape[1] // HEAD_WIDTH
    even = info[EVEN] == 1
    x1, x2, x3, y1, y2 = seats_of(l1k, c2k, t3)
    seats = ((x3, y2), (x2, y1), (x1, mate))
    row = lax.broadcasted_iota(jnp.int32, (BACK * SEAT, 1), 0)
    token = row % SEAT - 8
    position = (info[BLOCK] - BACK + row // SEAT) * AUDIO_ROWS + token
    asking = (
        (token >= 0) & (token < AUDIO_ROWS) & (position >= 0)
        & (jnp.abs(position - info[CENTER]) <= AUD_REACH)
    )

    def lead(h):
        c = cols(h)
        return dot_nt(jnp.concatenate([pick(even, *seat, c) for seat in seats]), kn[:, c])

    for h, x in ahead_of(list(range(heads)), lead):
        x = x * SCALE2
        peak = jnp.max(x, axis=1, keepdims=True)
        w = jnp.exp2(x - peak)
        mass = jnp.sum(w, axis=1, keepdims=True)
        mean = dot_nn(w.astype(BF16), v[:, cols(h)]) / mass
        weight = jnp.where(asking, peak + jnp.log2(mass), MASKED)
        half = slice((h % 2) * HEAD_WIDTH, (h % 2 + 1) * HEAD_WIDTH)
        for msg, j in ((m3, 0), (m2, 1), (m1, 2)):
            for i in range(AUDIO_ROWS):
                r, to = SEAT * j + 8 + i, i * (heads // 2) + h // 2
                msg[to : to + 1, half] = mean[r : r + 1]
            r = SEAT * j + 8
            msg[2 * heads : 2 * heads + AUDIO_ROWS, h : h + 1] = weight[r : r + AUDIO_ROWS]


def cross_kernel(info, qn, g, an, mate, l1k, c2k, t3, stat, cross, dqx):
    del stat
    heads = qn.shape[1] // HEAD_WIDTH
    even = info[EVEN] == 1
    x1, x2, x3, y1, y2 = seats_of(l1k, c2k, t3)
    seats = ((x3, y2), (x2, y1), (x1, mate), (an, an), (mate, x1), (y1, x2), (y2, x3))
    row = lax.broadcasted_iota(jnp.int32, (8 * SEAT, 1), 0)
    token = row % SEAT
    position = (info[BLOCK] - BACK + row // SEAT) * AUDIO_ROWS + token
    linked = (
        (token < AUDIO_ROWS) & (row < 7 * SEAT) & (position >= 0) & (position < info[TOTAL_AUDIO])
        & (jnp.abs(position - info[CENTER]) <= AUD_REACH)
    )

    def lead(h):
        c = cols(h)
        ak = jnp.concatenate([pick(even, *seat, c) for seat in seats] + [jnp.zeros((SEAT, HEAD_WIDTH), BF16)])
        av = pltpu.roll(ak.astype(F32), 8 * SEAT - 4, 0).astype(BF16)
        return ak, av, dot_nt(ak, qn[:, c]), dot_nt(av, g[:, c])

    for h, (ak, av, s, dp) in ahead_of(list(range(heads)), lead):
        c = cols(h)
        s = jnp.where(linked, s, MASKED)
        p = jnp.exp2((s - jnp.max(s, axis=0, keepdims=True)) * SCALE2)
        share = p * (1.0 / jnp.sum(p, axis=0, keepdims=True))
        rounded = share.astype(BF16)
        cross[c, :] = dot_tn(av, rounded)
        row_dot = jnp.sum(rounded.astype(F32) * dp, axis=0, keepdims=True)
        dqx[c, :] = dot_tn(ak, (share * (dp - row_dot)).astype(BF16))


def attend(lse, delta, s, dp):
    p = jnp.exp2(s * SCALE2 - lse)
    return p.astype(BF16), (p * (dp - delta)).astype(BF16)


def ahead_of(items, lead):
    ready = lead(items[0])
    for n, item in enumerate(items):
        now = ready
        if n + 1 < len(items):
            ready = lead(items[n + 1])
        yield item, now


def finish_queries(h, out, dq, cross, dqx, q_raw, gain, video, dn, total):
    c = cols(h)
    video[:, c] = (out + cross[c, :]).T.astype(BF16)
    d = ((dq + dqx[c, :]) * SCALE).T
    dn[:, c] = d
    term = q_raw[:, c].astype(F32) * gain[:, c] * d
    return term if total is None else total + term


def main_kernel(info, qn, g, kn, v, part, stat, out_p, a_p, b_p, l2, c3, cross, dqx, q_raw, gain, l3v,
                out_t, dq_t, dk, dv, video, dq, inner):
    del l3v
    l2k, l2v = halves(l2)
    c3k, c3v = halves(c3)
    heads = qn.shape[1] // HEAD_WIDTH
    even = info[EVEN] == 1
    live = jnp.where(even, info[LIVE + 1], info[LIVE + 2]) == 1

    def lead(h):
        c = cols(h)
        k = jnp.concatenate([pick(even, l2k, c3k, c), kn[:, c]])
        x = jnp.concatenate([pick(even, l2v, c3v, c), v[:, c]])
        return k[0:ROWS], x[0:ROWS], dot_nt(k, qn[:, c]), dot_nt(x, g[:, c])

    for h, (k, x, s, dp) in ahead_of(list(range(heads)), lead):
        c = cols(h)
        lse, delta = stat[h : h + 1, :], stat[heads + h : heads + h + 1, :]
        p, dlogit = attend(jnp.where(live, lse, -MASKED), delta, s[0:ROWS], dp[0:ROWS])
        own_p, own_dlogit = attend(lse, delta, s[ROWS:], dp[ROWS:])
        decay = jnp.exp2(part[h : h + 1, :] - lse)
        shift = part[heads + h : heads + h + 1, :] - delta
        out_t[c, :] = out_p[c, :] * decay + dot_tn(x, p)
        dq_t[c, :] = (a_p[c, :] + shift * b_p[c, :]) * decay + dot_tn(k, dlogit)
        dk[:, c] = dot_nn(own_dlogit, qn[:, c])
        dv[:, c] = dot_nn(own_p, g[:, c])
    inner[...] = jnp.zeros_like(inner)

    @when_odd(even)
    def _():
        total = None
        for h in range(heads):
            c = cols(h)
            total = finish_queries(h, out_t[c, :], dq_t[c, :], cross, dqx, q_raw, gain, video, dq, total)
        inner[0:1, :] = lane_sums(total)


def finish_keys(h, dk, dv, k_raw, gain, gv, dn, total):
    c = cols(h)
    d = dk * SCALE
    dn[:, c] = d
    gv[:, c] = dv.astype(BF16)
    term = k_raw[:, c].astype(F32) * gain[:, c] * d
    return term if total is None else total + term


def key_kernel(info, kn, v, n1, n2, n3, l1k, l1v, c1, l2, c2k, c2v, c3, dk_in, dv_in, k_raw, gain, inner_q, video_in,
               dk_out, dv_out, gv, inner, video, sem):
    c1k, c1v = halves(c1)
    l2k, l2v = halves(l2)
    c3k, c3v = halves(c3)
    heads = kn.shape[1] // HEAD_WIDTH
    even = info[EVEN] == 1

    @when_odd(even)
    def _():
        pltpu.make_async_copy(video_in, video, sem).start()

    l1k, c2k = top(l1k), top(c2k)
    queries = ((c1k, l1k), (c2k, l2k))
    grads = ((c1v, l1v), (c2v, l2v))
    stats = (None, n1, n2)
    items = [(h, t) for h in range(heads) for t in range(1, BACK)]

    def lead(item):
        h, t = item
        c = cols(h)
        q, o = pick(even, *queries[t - 1], c), pick(even, *grads[t - 1], c)
        return q, o, dot_nt(kn[:, c], q), dot_nt(v[:, c], o)

    for (h, t), (q, o, s, dp) in ahead_of(items, lead):
        c = cols(h)
        lse = jnp.where(info[AHEAD + t - 1] == 1, stats[t][h : h + 1, :], -MASKED)
        p, dlogit = attend(lse, stats[t][heads + h : heads + h + 1, :], s, dp)
        x, y = dot_nn(dlogit, q), dot_nn(p, o)
        dk, dv = (dk_in[:, c] + x, dv_in[:, c] + y) if t == 1 else (dk + x, dv + y)
        if t == BACK - 1:
            dk_out[:, cols(h)] = dk
            dv_out[:, cols(h)] = dv
    inner[...] = inner_q[...]

    @pl.when(even)
    def _():
        def lead(h):
            c = cols(h)
            return dot_nt(kn[:, c], c3k[:, c]), dot_nt(v[:, c], c3v[:, c])

        total = None
        for h, (s, dp) in ahead_of(list(range(heads)), lead):
            c = cols(h)
            lse = jnp.where(info[AHEAD + 2] == 1, n3[h : h + 1, :], -MASKED)
            p, dlogit = attend(lse, n3[heads + h : heads + h + 1, :], s, dp)
            dk = dk_out[:, c] + dot_nn(dlogit, c3k[:, c])
            dv = dv_out[:, c] + dot_nn(p, c3v[:, c])
            total = finish_keys(h, dk, dv, k_raw, gain, gv, dk_out, total)
        inner[0:1, :] = lane_sums(total)

    @when_odd(even)
    def _():
        pltpu.make_async_copy(video_in, video, sem).wait()


def final_kernel(info, qn, g, kn, v, stat, n3, l3k, l3v, out_t, dq_t, dk_in, dv_in, cross, dqx, gv_in,
                 q_raw, k_raw, gq, gk, result, gv, dn, inner, sem):
    heads = qn.shape[1] // HEAD_WIDTH
    even = info[EVEN] == 1

    @pl.when(even)
    def _():
        pltpu.make_async_copy(gv_in, gv, sem).start()

    inner[...] = jnp.zeros_like(inner)
    every = list(range(heads))

    @pl.when(even)
    def _():
        def lead(h):
            c = cols(h)
            return dot_nt(l3k[:, c], qn[:, c]), dot_nt(l3v[:, c], g[:, c])

        total = None
        for h, (s, dp) in ahead_of(every, lead):
            c = cols(h)
            lse = jnp.where(info[LIVE + 2] == 1, stat[h : h + 1, :], -MASKED)
            p, dlogit = attend(lse, stat[heads + h : heads + h + 1, :], s, dp)
            out = out_t[c, :] + dot_tn(l3v[:, c], p)
            dq = dq_t[c, :] + dot_tn(l3k[:, c], dlogit)
            total = finish_queries(h, out, dq, cross, dqx, q_raw, gq, result, dn, total)
        inner[0:1, :] = lane_sums(total)

    @when_odd(even)
    def _():
        def lead(h):
            c = cols(h)
            return dot_nt(kn[:, c], l3k[:, c]), dot_nt(v[:, c], l3v[:, c])

        total = None
        for h, (s, dp) in ahead_of(every, lead):
            c = cols(h)
            lse = jnp.where(info[AHEAD + 2] == 1, n3[h : h + 1, :], -MASKED)
            p, dlogit = attend(lse, n3[heads + h : heads + h + 1, :], s, dp)
            dk = dk_in[:, c] + dot_nn(dlogit, l3k[:, c])
            dv = dv_in[:, c] + dot_nn(p, l3v[:, c])
            total = finish_keys(h, dk, dv, k_raw, gk, result, dn, total)
        inner[0:1, :] = lane_sums(total)

    @pl.when(even)
    def _():
        pltpu.make_async_copy(gv_in, gv, sem).wait()


def norm_back(row, raw, gain, dn, e0, e1, i0, i1, out, part=None):
    f = factors(e0, e1)[row : row + 1]
    inner = i0[0:1, :] + i1[0:1, :]
    fr = as_rows(f)
    back = as_rows(f * f * f * inner / D)
    heads = raw.shape[1] // HEAD_WIDTH
    for h in range(heads) if part is None else range(part * heads // 2, (part + 1) * heads // 2):
        c = cols(h)
        out[:, c] = (fr * gain[:, c] * dn[:, c] - raw[:, c].astype(F32) * back).astype(BF16)


def late_kernel(info, q, k, gq, gk, dn, e0, e1, i0, i1, gq_in, gk_in, grad_q, grad_k, held, sems):
    del gq_in, gk_in
    even = info[EVEN] == 1
    half = held.shape[1] // 2

    def fill(row, raw, gain, out):
        for i in range(2):
            c = pl.ds(i * half, half)
            norm_back(row, raw, gain, dn, e0, e1, i0, i1, held, i)
            pltpu.make_async_copy(held.at[:, c], out.at[:, c], sems.at[i]).start()

    @pl.when(even)
    def _():
        fill(0, q, gq, grad_q)

    @when_odd(even)
    def _():
        fill(1, k, gk, grad_k)

    for i in range(2):
        c = pl.ds(i * half, half)
        pltpu.make_async_copy(held.at[:, c], grad_q.at[:, c], sems.at[i]).wait()


def shadow_kernel(info, kn, v, an, mate, t3, l1k, l1v, c1, l2, c2k, c2v, l3k, l3v, c3, r1, r2, r3,
                  q, k, gq, gk, dq, dk, e0, e1, i0, i1, result, video_in, gv_in,
                  out, video, gv, grad_q, grad_k, held, grad, sems):
    c1k, c1v = halves(c1)
    l2k, l2v = halves(l2)
    t1, t2, t3, u1, u2 = seats_of(l1k, c2k, t3)
    l1k, c2k = top(l1k), top(c2k)
    c3k, c3v = halves(c3)
    heads = kn.shape[1] // HEAD_WIDTH
    even, block = info[EVEN] == 1, info[BLOCK]
    del video_in, gv_in

    @pl.when(even)
    def _():
        pltpu.make_async_copy(result, video, sems.at[0]).start()
        norm_back(1, k, gk, dk, e0, e1, i0, i1, grad)
        pltpu.make_async_copy(grad, grad_k, sems.at[1]).start()

    @when_odd(even)
    def _():
        pltpu.make_async_copy(result, gv, sems.at[0]).start()
        norm_back(0, q, gq, dq, e0, e1, i0, i1, grad)
        pltpu.make_async_copy(grad, grad_q, sems.at[1]).start()

    keys = ((l1k, c1k), (l2k, c2k), (l3k, c3k))
    values = ((l1v, c1v), (l2v, c2v), (l3v, c3v))
    token = lax.broadcasted_iota(jnp.int32, (SEAT, 1), 0) - 8
    asks = (token >= 0) & (token < AUDIO_ROWS)
    linked = [asks & (jnp.abs(block * AUDIO_ROWS + token - info[CENTER]) <= AUD_REACH)]
    c = cols(0)
    for t, (first, second) in enumerate(((t1, mate), (t2, u1), (t3, u2))):
        seat = jnp.where(even, first[:, c], second[:, c]).astype(F32)
        gap = (token + AUDIO_ROWS * (t + 1) - 2).astype(F32) - seat[12:13, 0:1]
        linked.append(asks & (block - t - 1 >= 0) & (jnp.abs(gap) <= AUD_REACH))

    def lead(h):
        c = cols(h)
        k = jnp.concatenate([kn[:, c]] + [pick(even, *pair, c) for pair in keys])
        x = dot_nt(an[:, c], k) * SCALE2
        return [jnp.where(m, x[:, t * ROWS : (t + 1) * ROWS], MASKED) for t, m in enumerate(linked)]

    for h, found in ahead_of(list(range(heads)), lead):
        c = cols(h)
        peak = jnp.maximum(jnp.maximum(found[0], found[1]), jnp.maximum(found[2], found[3]))
        peak = jnp.max(peak, axis=1, keepdims=True)
        ws = [jnp.exp2(x - peak) for x in found]
        mass = jnp.sum((ws[0] + ws[1]) + (ws[2] + ws[3]), axis=1, keepdims=True)
        w = jnp.concatenate([x.astype(BF16) for x in ws], axis=1)
        x = jnp.concatenate([v[:, c]] + [pick(even, *pair, c) for pair in values])
        held[0:SEAT, c] = dot_nn(w, x) / mass
        held[SEAT : 2 * SEAT, c] = jnp.broadcast_to(peak + jnp.log2(mass), (SEAT, HEAD_WIDTH))
    for d, r in enumerate((r1, r2, r3)):
        base = 2 * SEAT + SEAT * d
        for i in range(AUDIO_ROWS):
            for j in range(heads // 2):
                at = 2 * heads + i * (heads // 2) + j
                held[base + i : base + i + 1, 2 * j * HEAD_WIDTH : 2 * (j + 1) * HEAD_WIDTH] = r[at : at + 1, :]
        w = jnp.where(info[AHEAD + d] == 1, r[4 * heads : 4 * heads + 8, 0:HEAD_WIDTH], MASKED)
        for h in range(heads):
            held[base + 8 : base + SEAT, cols(h)] = jnp.broadcast_to(w[:, h : h + 1], (8, HEAD_WIDTH))
    for h in range(heads):
        c = cols(h)
        means, weights = [held[8:12, c]], [held[SEAT + 8 : SEAT + 12, c]]
        for d in range(BACK):
            base = 2 * SEAT + SEAT * d
            means.append(held[base : base + 4, c])
            weights.append(held[base + 8 : base + 12, c])
        out[:, c] = merged(means, weights)[0].astype(BF16)
    pltpu.make_async_copy(result, video, sems.at[0]).wait()
    pltpu.make_async_copy(grad, grad_q, sems.at[1]).wait()


def on_device(
    video_query, video_key, video_value, audio_query, audio_key, audio_value,
    video_query_gain, video_key_gain, audio_query_gain, audio_key_gain,
    tile_flags, audio_centers, out_grad,
):
    blocks = lax.axis_size("ctx")
    width = video_query.shape[1]
    heads = width // HEAD_WIDTH
    block = lax.axis_index("ctx").astype(jnp.int32)

    link1 = [(i, i + 1) for i in range(1, blocks - 1, 2)] + [(i + 1, i) for i in range(1, blocks - 1, 2)]
    link2 = [(i, i + 2) for i in range(0, blocks - 2, 2)] + [(i, i - 2) for i in range(3, blocks, 2)]
    link3 = [(i, i + 3) for i in range(1, blocks - 3, 2)] + [(i, i - 3) for i in range(4, blocks, 2)]
    chip = [(i, i + 1) for i in range(0, blocks, 2)] + [(i + 1, i) for i in range(0, blocks, 2)]
    forward = [(i, i + 1) for i in range(1, blocks - 1, 2)]

    def send(x, pairs):
        return lax.ppermute(x, "ctx", pairs)

    def back(x, by):
        return send(x, [(i, i - by) for i in range(by, blocks)])

    def swap(x):
        return lax.ppermute(x, "tp", [(0, 1), (1, 0)])

    steps = jnp.arange(BACK, dtype=jnp.int32)
    info = jnp.concatenate([
        (1 - block % 2)[None],
        tile_flags[0] * (block - 1 - steps >= 0),
        block[None],
        audio_centers,
        (block + 1 + steps < blocks).astype(jnp.int32),
        jnp.full((7,), blocks * AUDIO_ROWS, jnp.int32),
    ]).astype(jnp.int32)
    relative = (audio_centers[0] - (block * AUDIO_ROWS + AUDIO_ROWS // 2)).astype(BF16)
    audio = jnp.concatenate([
        audio_key, audio_value, audio_query, jnp.full((AUDIO_ROWS, width), relative, BF16)
    ])
    gq, gk, gaq, gak = (g[None, :] for g in (video_query_gain, video_key_gain, audio_query_gain, audio_key_gain))

    full = ((ROWS, width), BF16)
    wide = ((ROWS, width), F32)
    turned = ((width, ROWS), F32)
    pair = ((2 * ROWS, width), BF16)
    small = ((8, ROWS), F32)
    mail = ((2 * heads + 8, ROWS), F32)
    stats = ((2 * heads, ROWS), F32)
    letter = ((4 * heads + 8, ROWS), F32)

    def after(x, *done):
        return lax.optimization_barrier((x, *done))[0]

    (xv,) = call(
        first_kernel, [full], [HBM, HBM], [pltpu.SemaphoreType.DMA(())], name="first", limit=LOAD_LIMIT
    )(video_value, out_grad)
    l1v = send(xv, link1)
    mate = send(audio, chip)

    energy, q, k = call(
        energy_kernel, [small, full, full], [VMEM] * 4, [pltpu.VMEM((128, 128), F32)], name="energy"
    )(video_query, video_key, audio, mate)
    peer = swap(energy)
    v, g = call(
        load_kernel, [full, full], [HBM, HBM, VMEM], [pltpu.SemaphoreType.DMA((2,))], name="load"
    )(video_value, out_grad, energy)
    seat = ((SEAT, width), BF16)
    qn, kn, an, mate, xk, both = call(
        prep_kernel, [full, full, seat, seat, ((ROWS + 2 * SEAT, width), BF16), pair],
        [SMEM] + [VMEM] * 12 + [HBM], name="prep",
    )(info, q, k, v, g, audio, mate, energy, peer, gq, gk, gaq, gak, l1v)

    l1k, c1, c2v = send(xk, link1), send(both, chip), send(l1v, chip)
    part, out_p, a_p, b_p = call(
        own_kernel, [stats, turned, turned, turned], [SMEM] + [VMEM] * 5 + [HBM], name="own",
    )(info, qn, g, kn, v, c1, c2v)
    l2 = send(after(both, c1), link2)
    l1k, _ = lax.optimization_barrier((l1k, part))
    c2k = send(l1k, chip)
    (lk,) = call(strip_kernel, [full], [VMEM], name="strip")(l1k)
    part, helper, out_p, a_p, b_p = call(
        next_kernel, [stats, stats, turned, turned, turned], [SMEM] + [VMEM] * 10, [pltpu.VMEM((48, ROWS), F32)],
        name="next", same={8: 2, 9: 3, 10: 4},
    )(info, qn, g, l1k, l1v, c2k, c2v, part, out_p, a_p, b_p)
    helped = send(helper, forward)
    t3 = send(after(an, part), link3)
    l2, lk, lv, t3, _, _ = lax.optimization_barrier((l2, lk, l1v, t3, part, helped))
    c3 = send(l2, chip)
    l3v = send(lv, link2)
    m1, m2, m3 = call(mail_kernel, [mail] * 3, [SMEM] + [VMEM] * 6 + [HBM], name="mail")(
        info, kn, v, mate, l1k, c2k, t3, l2
    )
    stat, s1, s2, s3 = call(
        stat_kernel, [stats, letter, letter, letter], [SMEM] + [VMEM] * 9,
        [pltpu.VMEM((2 * heads, ROWS), F32), pltpu.VMEM((48, ROWS), F32)],
        name="stat",
    )(info, qn, g, l2, c3, part, helped, m1, m2, m3)
    n1, n2, n3 = back(s1, 1), back(s2, 2), back(s3, 3)
    cross, dqx = call(cross_kernel, [turned, turned], [SMEM] + [VMEM] * 7 + [HBM], name="cross")(
        info, qn, g, an, mate, l1k, c2k, t3, stat
    )
    out_t, dq_t, dk, dv, video, dq, inner_q = call(
        main_kernel, [turned, turned, wide, wide, full, wide, small], [SMEM] + [VMEM] * 15 + [HBM],
        name="main",
    )(info, qn, g, kn, v, part, stat, out_p, a_p, b_p, l2, c3, cross, dqx, q, gq, l3v)
    l3k = send(after(lk, l3v, n1, n2, n3, cross), link2)
    dk, dv, value, inner, video = call(
        key_kernel, [wide, wide, full, small, full], [SMEM] + [VMEM] * 18, [pltpu.SemaphoreType.DMA(())],
        name="key", same={13: 0, 14: 1}, out_specs=[VMEM] * 4 + [HBM],
    )(info, kn, v, n1, n2, n3, l1k, l1v, c1, l2, c2k, c2v, c3, dk, dv, k, gk, inner_q, video)
    inner_peer = swap(inner)
    result, value, dn, last = call(
        final_kernel, [full, full, wide, small], [SMEM] + [VMEM] * 19, [pltpu.SemaphoreType.DMA(())],
        name="final", out_specs=[VMEM, HBM, VMEM, VMEM],
    )(info, qn, g, kn, v, stat, n3, l3k, l3v, out_t, dq_t, dk, dv, cross, dqx, value, q, k, gq, gk)
    last_peer = swap(last)
    audio_out, video, value, grad_query, grad_key = call(
        shadow_kernel, [((AUDIO_ROWS, width), BF16)] + [full] * 4, [SMEM] + [VMEM] * 28 + [HBM] * 2,
        [
            pltpu.VMEM((5 * SEAT, width), F32), pltpu.VMEM((ROWS, width), BF16),
            pltpu.SemaphoreType.DMA((2,)),
        ],
        name="shadow", out_specs=[VMEM] + [HBM] * 4, same={29: 1, 30: 2},
    )(
        info, kn, v, an, mate, t3, l1k, l1v, c1, l2, c2k, c2v, l3k, l3v, c3, n1, n2, n3,
        q, k, gq, gk, dq, dk, energy, peer, inner, inner_peer, result, video, value,
    )
    grad_query, grad_key = call(
        late_kernel, [full, full], [SMEM] + [VMEM] * 9 + [HBM] * 2,
        [pltpu.VMEM((ROWS, width), BF16), pltpu.SemaphoreType.DMA((2,))],
        name="late", same={10: 0, 11: 1}, out_specs=[HBM] * 2,
    )(info, q, k, gq, gk, dn, energy, peer, last, last_peer, grad_query, grad_key)
    return (video, audio_out, grad_query, grad_key, value)


def solution(mesh):
    rows = P("ctx", "tp")
    return jax.shard_map(
        on_device,
        mesh=mesh,
        in_specs=(rows,) * 6 + (P("tp"),) * 4 + (P("ctx", None), P("ctx"), rows),
        out_specs=(rows,) * 5,
        check_vma=False,
    )
```
